256 devices in a mesh: lon: 16 (over y_hi, x, core), tm: 16 (over y_lo, z).
Axes of the slice: x: 4, y: 4 (y_hi: 2, y_lo: 2; y = y_hi * 2 + y_lo), z: 8, core: 2. Of those that a mesh axis runs over, the one named last changes fastest.
Arguments:
- frames_in: bfloat16 [64, 32, 64, 1536], P('tm', None, 'lon'), may hold values from -6 to 6
- conv_kernel: float32 [3, 3, 1536], replicated, may hold values from -2 to 2
- w_query: bfloat16 [1536, 768], replicated, may hold values from -0.15625 to 0.15625
- w_key: bfloat16 [1536, 768], replicated, may hold values from -0.15625 to 0.15625
- w_value: bfloat16 [1536, 768], replicated, may hold values from -0.15625 to 0.15625
- w_out: bfloat16 [768, 1536], replicated, may hold values from -0.21875 to 0.21875
- norm_gain: float32 [768], replicated, may hold values from 0.1 to 1.9
- log_gate: float32 [64, 6], P('tm'), may hold values from -2.5 to 0
- cam_valid: int32 [64, 6], P('tm'), may hold values 0 or 1
- live_frames: int32 [16], P('tm'), may hold values from 2 to 4, as said below
Outputs:
- mixed_out: bfloat16 [64, 32, 64, 1536], P('tm', None, 'lon')
The draws below stay inside these ranges and needn't reach their ends.
Inputs may be any that keep to these rules, and one draw needn't show every extreme that they name: Frames of a slab from live_frames on are padding; in every draw some slab has all 4 frames live.
All inputs are finite; a program needn't handle non-finite values. No bound on the sum of `cam_valid` on one device may be relied on, other than what follows from the above.
Results may differ from the reference program's by a relative error of at most 0.011.
Values may be sent and summed in bfloat16 or wider, within the bound.
A program may use at most 64 MiB of HBM per device.

```python
import math
import jax
import jax.numpy as jnp
from jax import lax

D = 1536
HEADS = 6
HD = 128
CAMS = 6
LAT = 32
FR_DEV = 4
HK = 768
WINDOW_FRAMES = 64
LONG = 64
SLABS = 16


def draw_log_gate(key, part):
    key = jax.random.fold_in(key, 7)
    segment_random_keys = jax.random.split(key, 6)
    fast_share = 0.5
    random_wobble = jnp.exp(jnp.clip(0.35 * jax.random.normal(segment_random_keys[5], (WINDOW_FRAMES, HEADS), jnp.float32), -math.log(2.0), math.log(2.0)))
    fast_heads = jax.random.uniform(segment_random_keys[0], (HEADS,), jnp.float32) < fast_share
    sluggish_decay_rate = jax.random.uniform(segment_random_keys[1], (HEADS,), jnp.float32, 0.15, 0.45) * (math.log(10.0) / WINDOW_FRAMES)
    fast_rate = jax.random.uniform(segment_random_keys[2], (WINDOW_FRAMES, HEADS), jnp.float32, 1.0, 2.5)
    sudden_spikes = jax.random.uniform(segment_random_keys[3], (WINDOW_FRAMES, 1), jnp.float32) < 3.0 / WINDOW_FRAMES
    spike_penalty = jnp.log(jax.random.uniform(segment_random_keys[4], (WINDOW_FRAMES, 1), jnp.float32, 0.6, 0.8))
    sluggish_log_decay = -sluggish_decay_rate[None, :] * random_wobble + jnp.where(sudden_spikes, spike_penalty, 0.0)
    return jnp.where(fast_heads[None, :], -fast_rate, sluggish_log_decay).astype(jnp.float32)


def draw_live_frames(key, part):
    key = jax.random.fold_in(key, 5)
    first_key, second_key = jax.random.split(key)
    counts = jax.random.randint(first_key, (SLABS,), FR_DEV // 2, FR_DEV + 1)
    filled = jax.random.randint(second_key, (), 0, SLABS)
    return jnp.where(jnp.arange(SLABS) == filled, FR_DEV, counts).astype(jnp.int32)


def plant(array, stream_key, low, high):
    longest = array.shape.index(max(array.shape))
    spots = []
    for shift in (0, 1):
        where = [jax.random.randint(jax.random.fold_in(stream_key, axis), (), 0, length) for axis, length in enumerate(array.shape)]
        where[longest] = (where[longest] + shift) % array.shape[longest]
        spots.append(tuple(where))
    return array.at[spots[0]].set(low).at[spots[1]].set(high)


def steps_of(rng, dims, cuts, smallest, top_value):
    def one(dim, shards_of):
        steps = jax.random.uniform(jax.random.fold_in(jax.random.fold_in(rng, 6), dim), (shards_of,), jnp.float32, smallest / len(cuts), top_value / len(cuts))
        return jnp.repeat(jnp.exp(steps), dims[dim] // shards_of).reshape((-1,) + (1,) * (len(dims) - dim - 1))

    factor_of = one(*cuts[0])
    for cut in cuts[1:]:
        factor_of = factor_of * one(*cut)
    return factor_of


def centred(stream_key, extent, width, bound, cuts=(), kind=jnp.bfloat16):
    entries = width * jax.random.normal(stream_key, extent, jnp.float32)
    if cuts:
        entries = entries * steps_of(stream_key, extent, cuts, -0.22, 0.18)
    return jnp.clip(entries, -bound, bound).astype(kind)


def setup_inputs(seed: int = 0) -> dict:
    streams_of = jax.random.split(jax.random.key(seed), 11)
    frames_in = centred(streams_of[0], (WINDOW_FRAMES, LAT, LONG, D), 1.0, 6.0, ((0, 16), (2, 16)))
    conv_kernel = centred(streams_of[1], (3, 3, D), 0.35, 2.0, (), jnp.float32)
    w_query = centred(streams_of[2], (D, HK), D ** -0.5, 0.15625)
    w_key = centred(streams_of[3], (D, HK), D ** -0.5, 0.15625)
    w_value = centred(streams_of[4], (D, HK), D ** -0.5, 0.15625)
    w_out = centred(streams_of[5], (HK, D), HK ** -0.5, 0.21875)
    norm_gain = jnp.clip(1.0 + 0.18 * jax.random.normal(streams_of[6], (HK,), jnp.float32), 0.1, 1.9)
    log_gate = draw_log_gate(jax.random.fold_in(streams_of[10], 71), 0)
    cam_valid = plant((jax.random.randint(streams_of[8], (WINDOW_FRAMES, CAMS), 0, 6) < 4).astype(jnp.int32), jax.random.fold_in(streams_of[8], 1), 0, 1)
    live_frames = draw_live_frames(jax.random.fold_in(streams_of[10], 71), 0)
    return {"frames_in": frames_in, "conv_kernel": conv_kernel, "w_query": w_query, "w_key": w_key, "w_value": w_value, "w_out": w_out, "norm_gain": norm_gain, "log_gate": log_gate, "cam_valid": cam_valid, "live_frames": live_frames}


def conv_frame(frame_cells, conv_kernel):
    padded = jnp.pad(frame_cells.astype(jnp.float32), ((1, 1), (0, 0), (0, 0)))
    filtered = jnp.zeros((LAT, LONG, D), jnp.float32)
    for lat_tap in range(3):
        lat_rows = padded[lat_tap:lat_tap + LAT]
        for lon_tap in range(3):
            filtered = filtered + conv_kernel[lat_tap, lon_tap] * jnp.roll(lat_rows, 1 - lon_tap, axis=1)
    return jax.nn.silu(filtered).astype(jnp.bfloat16)

def reference(frames_in, conv_kernel, w_query, w_key, w_value, w_out, norm_gain, log_gate, cam_valid, live_frames):
    columns = jnp.arange(LONG).astype(jnp.int32)
    camera = columns * CAMS // LONG
    onehot = (camera[None, :] == jnp.arange(CAMS).astype(jnp.int32)[:, None]).astype(jnp.float32)
    visible = jnp.dot(cam_valid.astype(jnp.float32), onehot, precision=lax.Precision.HIGHEST)
    frame_ids = jnp.arange(WINDOW_FRAMES).astype(jnp.int32)
    frame_live = (frame_ids % FR_DEV < live_frames[frame_ids // FR_DEV]).astype(jnp.float32)
    key_keep = visible * frame_live[:, None]

    def project(inputs):
        frame_cells, keep_row = inputs
        mixed = conv_frame(frame_cells, conv_kernel).reshape(LAT * LONG, D)
        queries = jnp.dot(mixed, w_query, preferred_element_type=jnp.float32).astype(jnp.bfloat16)
        keys = jnp.dot(mixed, w_key, preferred_element_type=jnp.float32).astype(jnp.bfloat16)
        values = jnp.dot(mixed, w_value, preferred_element_type=jnp.float32).astype(jnp.bfloat16)
        keys = keys.reshape(LAT, LONG, HEADS, HD) * keep_row[None, :, None, None].astype(jnp.bfloat16)
        state_terms = jnp.einsum('nhd,nhe->hde', keys.reshape(-1, HEADS, HD).astype(jnp.float32), values.reshape(-1, HEADS, HD).astype(jnp.float32), precision=lax.Precision.HIGHEST)
        return (queries, state_terms)
    queries, state_terms = lax.map(project, (frames_in, key_keep))
    frame_rates = log_gate * frame_live[:, None]

    def recur(carried, inputs):
        rate_row, frame_term = inputs
        carried = jnp.exp(rate_row)[:, None, None] * carried + frame_term
        return (carried, carried.astype(jnp.bfloat16))
    _, state_rounded = lax.scan(recur, jnp.zeros((HEADS, HD, HD), jnp.float32), (frame_rates, state_terms))

    def output(inputs):
        query_rows, state_frame, alive = inputs
        readout = jnp.einsum('nhd,hde->nhe', query_rows.reshape(-1, HEADS, HD).astype(jnp.float32), state_frame.astype(jnp.float32), precision=lax.Precision.HIGHEST)
        inverse_rms = lax.rsqrt(lax.optimization_barrier(jnp.mean(readout * readout, axis=-1, keepdims=True)) + 1e-05)
        normed = (readout * inverse_rms * norm_gain.reshape(HEADS, HD)).astype(jnp.bfloat16).reshape(-1, HK)
        result = jnp.dot(normed, w_out, preferred_element_type=jnp.float32) * alive
        return result.reshape(LAT, LONG, D).astype(jnp.bfloat16)
    return lax.map(output, (queries, state_rounded, frame_live))
```

```python
import functools

import jax
import jax.numpy as jnp
from jax import lax
from jax.experimental import pallas as pl
from jax.experimental.pallas import tpu as pltpu
from jax.sharding import PartitionSpec as P

MESH = pl.DeviceIdType.MESH
F32 = jnp.float32
BF16 = jnp.bfloat16

HEADS = 6
HD = 128
CAMS = 6
FRAMES = 4
LAT = 32
COLS = 4
D = 1536
HK = HEADS * HD
TOK = LAT * COLS
LONG = 64
CHUNK = 256
HALF = FRAMES * 2 * LAT
OWN = HK // 2
CHIPS = 8
PIECE = OWN // CHIPS
SLABS = 16
LONS = 16


def repeat(first, last, body):
    def step(i, carry):
        body(i)
        return carry

    lax.fori_loop(first, last, step, 0)


def dot(a, b):
    return jnp.dot(a, b, preferred_element_type=F32)


def column_of(t):
    block = t // LAT
    return jnp.where(block == 0, 1, jnp.where(block == 1, 2, jnp.where(block == 2, 0, 3)))


def kernel(
    x_hbm,
    ck_hbm,
    wq_hbm,
    wk_hbm,
    wv_hbm,
    wo_hbm,
    gain_hbm,
    lg_hbm,
    cam_hbm,
    live_ref,
    out_hbm,
    x_v,
    ck,
    wq,
    wk,
    wv,
    wo,
    gain,
    lg,
    cam,
    shift3,
    shift_h,
    order,
    edge_out,
    edge_in,
    partial,
    mixed,
    q_v,
    k_v,
    v_v,
    keep,
    dec,
    reach,
    other,
    own,
    abuf,
    bsend,
    bbuf,
    tmsg,
    tbuf,
    tdec,
    states,
    inc,
    normed,
    out_v,
    load_sem,
    out_sem,
    halo_send,
    halo_recv,
    a_send,
    a_recv,
    b_send,
    b_recv,
    t_send,
    t_recv,
    c_send,
    c_recv,
    d_send,
    d_recv,
    i_send,
    i_recv,
):
    lon = lax.axis_index("lon")
    slab = lax.axis_index("tm")
    core = lon % 2
    chip = lon // 2
    partner = lon + 1 - 2 * core
    mine = pl.multiple_of(core * OWN + chip * PIECE, 16)
    mine_own = pl.multiple_of(chip * PIECE, 16)

    loads = []
    for n, (src, dst) in enumerate(
        (
            (x_hbm, x_v),
            (ck_hbm, ck),
            (lg_hbm, lg),
            (cam_hbm, cam),
            (gain_hbm, gain),
            (wk_hbm, wk),
            (wv_hbm, wv),
            (wq_hbm, wq),
            (wo_hbm, wo),
        )
    ):
        copy = pltpu.make_async_copy(src, dst, load_sem.at[n])
        copy.start()
        loads.append(copy)
    l_x, l_ck, l_lg, l_cam, l_gain, l_wk, l_wv, l_wq, l_wo = loads

    barrier = pltpu.get_barrier_semaphore()

    def greet(d):
        pl.semaphore_signal(
            barrier, inc=1, device_id={"lon": (lon + d) % LONS}, device_id_type=MESH
        )
        pl.semaphore_signal(
            barrier, inc=1, device_id={"tm": (slab + d) % SLABS}, device_id_type=MESH
        )

    repeat(1, LONS, greet)

    row = lax.broadcasted_iota(jnp.int32, (TOK, TOK), 0)
    col = lax.broadcasted_iota(jnp.int32, (TOK, TOK), 1)
    c_row = column_of(row)
    for i in range(3):
        lat = row % LAT + (i - 1)
        hit = (lat >= 0) & (lat < LAT) & (col == lat * COLS + c_row)
        shift3[i * TOK : (i + 1) * TOK, :] = jnp.where(hit, 1.0, 0.0).astype(BF16)
    hit = row == (col % LAT) * COLS + column_of(col)
    order[...] = jnp.where(hit, 1.0, 0.0).astype(BF16)
    row = lax.broadcasted_iota(jnp.int32, (3 * LAT, LAT), 0)
    col = lax.broadcasted_iota(jnp.int32, (3 * LAT, LAT), 1)
    shift_h[...] = jnp.where(col == row % LAT + row // LAT - 1, 1.0, 0.0).astype(BF16)

    l_x.wait()
    x_rows = x_v.reshape(FRAMES * TOK, D)
    for f in range(FRAMES):

        def extract(j):
            lanes = pl.ds(pl.multiple_of(j * CHUNK, CHUNK), CHUNK)
            planes = dot(shift3[TOK + 2 * LAT : 2 * TOK, :], x_rows[f * TOK : (f + 1) * TOK, lanes])
            planes = planes.astype(BF16)
            edge_out[1, f, :, lanes] = planes[:LAT]
            edge_out[0, f, :, lanes] = planes[LAT:]

        repeat(0, D // CHUNK, extract)

    pl.semaphore_wait(barrier, 2 * (LONS - 1))
    halos = []
    for side, target in ((0, (lon + 1) % LONS), (1, (lon + LONS - 1) % LONS)):
        copy = pltpu.make_async_remote_copy(
            src_ref=edge_out.at[side],
            dst_ref=edge_in.at[side],
            send_sem=halo_send.at[side],
            recv_sem=halo_recv.at[side],
            device_id={"lon": target},
            device_id_type=MESH,
        )
        copy.start()
        halos.append(copy)

    l_lg.wait()
    l_cam.wait()
    n_live = live_ref[0]
    frame = lax.broadcasted_iota(jnp.int32, (FRAMES, HEADS), 0)
    live = jnp.where(frame < n_live, 1.0, 0.0).astype(F32)
    decay = jnp.exp(lg[...] * live)
    sofar = decay[0:1]
    for f in range(FRAMES):
        if f:
            sofar = sofar * decay[f : f + 1]
        for h in range(HEADS):
            at = f * HEADS + h
            dec[at : at + 1, :] = jnp.broadcast_to(decay[f : f + 1, h : h + 1], (1, HD))
            reach[at : at + 1, :] = jnp.broadcast_to(sofar[:, h : h + 1], (1, HD))
    valid = cam[...].astype(F32) * live
    lane = lax.broadcasted_iota(jnp.int32, (1, CAMS), 1)
    for n, c in enumerate((1, 2, 0, 3)):
        camera = ((lon * COLS + c) * CAMS) // LONG
        for f in range(FRAMES):
            bit = jnp.sum(jnp.where(lane == camera, valid[f : f + 1], 0.0), axis=1, keepdims=True)
            at = f * 2 * LAT + (n % 2) * LAT
            keep[n // 2, at : at + LAT, :] = jnp.broadcast_to(bit, (LAT, HD))

    l_ck.wait()

    def taps(j):
        lanes = pl.ds(pl.multiple_of(j * CHUNK, CHUNK), CHUNK)
        k = [[0.5 * ck[i, n : n + 1, lanes] for n in range(3)] for i in range(3)]

        def one(f):
            x = x_rows[pl.ds(pl.multiple_of(f * TOK, TOK), TOK), lanes]
            s = [dot(shift3[i * TOK : (i + 1) * TOK, :], x) for i in range(3)]
            place = {1: 0, 2: 1, 0: 2, 3: 3}

            def plane(i, c):
                at = place[c] * LAT
                return s[i][at : at + LAT]

            at = pl.multiple_of(f * 2 * LAT, 2 * LAT)
            for n, c in enumerate((1, 2, 0, 3)):
                total = None
                for i in range(3):
                    for m in range(3):
                        if 0 <= c + m - 1 < COLS:
                            term = k[i][m] * plane(i, c + m - 1)
                            total = term if total is None else total + term
                rows = pl.ds(at + (n % 2) * LAT, LAT)
                if n < 2:
                    mixed[0, rows, lanes] = (total * jnp.tanh(total) + total).astype(BF16)
                else:
                    partial[rows, lanes] = total

        repeat(0, FRAMES, one)

    repeat(0, D // CHUNK, taps)

    def project(half, weights, dst, masked):
        def one(j):
            lanes = pl.ds(pl.multiple_of(j * CHUNK, CHUNK), CHUNK)
            r = dot(mixed[half], weights[:, lanes])
            if masked:
                m = keep[half]
                r = r * jnp.concatenate([m, m], axis=1)
            dst[half, :, lanes] = r.astype(BF16)

        repeat(0, HK // CHUNK, one)

    l_wk.wait()
    project(0, wk, k_v, True)
    l_wv.wait()
    project(0, wv, v_v, False)
    l_wq.wait()
    project(0, wq, q_v, False)

    for copy in halos:
        copy.wait_recv()

    def edge_taps(j):
        lanes = pl.ds(pl.multiple_of(j * CHUNK, CHUNK), CHUNK)
        k = [[0.5 * ck[i, n : n + 1, lanes] for n in (0, 2)] for i in range(3)]

        def one(f):
            at = pl.multiple_of(f * 2 * LAT, 2 * LAT)
            for side in range(2):
                s = dot(shift_h[...], edge_in[side, f, :, lanes])
                rows = pl.ds(at + side * LAT, LAT)
                total = partial[rows, lanes]
                for i in range(3):
                    total = total + k[i][side] * s[i * LAT : (i + 1) * LAT]
                mixed[1, rows, lanes] = (total * jnp.tanh(total) + total).astype(BF16)

        repeat(0, FRAMES, one)

    repeat(0, D // CHUNK, edge_taps)
    project(1, wk, k_v, True)
    project(1, wv, v_v, False)

    def scan_head(h, put):
        lanes = pl.ds(pl.multiple_of(h * HD, HD), HD)
        carried = None
        for f in range(FRAMES):
            rows = pl.ds(f * 2 * LAT, 2 * LAT)
            keys = k_v[:, rows, lanes].reshape(TOK, HD)
            values = v_v[:, rows, lanes].reshape(TOK, HD)
            term = lax.dot_general(keys, values, (((0,), (0,)), ((), ())), preferred_element_type=F32)
            if f:
                term = term + dec[pl.ds(f * HEADS + h, 1), :] * carried
            carried = term
            put(f, term)

    def scan_other(n):
        def put(f, term):
            other[f, pl.ds(pl.multiple_of(n * HD, HD), HD), :] = term.astype(BF16)

        scan_head((1 - core) * 3 + n, put)

    def scan_own(n):
        def put(f, term):
            own[f, pl.ds(pl.multiple_of(n * HD, HD), HD), :] = term

        scan_head(core * 3 + n, put)

    repeat(0, 3, scan_other)
    LAST = pl.ds(FRAMES - 1, 1)
    REST = pl.ds(0, FRAMES - 1)
    parts = (LAST, REST)

    def a_copy(n):
        return pltpu.make_async_remote_copy(
            src_ref=other.at[parts[n]],
            dst_ref=abuf.at[parts[n]],
            send_sem=a_send.at[n],
            recv_sem=a_recv.at[n],
            device_id={"lon": partner},
            device_id_type=MESH,
        )

    for n in range(2):
        a_copy(n).start()
    repeat(0, 3, scan_own)

    def b_copy(n, d):
        to = (chip + d) % CHIPS
        return pltpu.make_async_remote_copy(
            src_ref=bsend.at[parts[n], pl.ds(pl.multiple_of(to * PIECE, 16), PIECE)],
            dst_ref=bbuf.at[d - 1, parts[n]],
            send_sem=b_send.at[n, d],
            recv_sem=b_recv.at[n],
            device_id={"lon": 2 * to + core},
            device_id_type=MESH,
        )

    for n, frames in enumerate(((FRAMES - 1,), tuple(range(FRAMES - 1)))):
        a_copy(n).wait_recv()
        for f in frames:

            def add(i, f=f):
                rows = pl.ds(pl.multiple_of(i * HD, HD), HD)
                total = own[f, rows, :] + abuf[f, rows, :].astype(F32)
                own[f, rows, :] = total
                bsend[f, rows, :] = total.astype(BF16)

            repeat(0, 3, add)
        repeat(1, CHIPS, lambda d, n=n: b_copy(n, d).start())

    whole = jnp.concatenate(
        [reach[(FRAMES - 1) * HEADS :, :], jnp.zeros((2, HD), F32)], axis=0
    )
    high = whole.astype(BF16)
    low = (whole - high.astype(F32)).astype(BF16)
    tmsg[PIECE:, :] = jnp.concatenate([high.astype(F32), low.astype(F32)], axis=0).astype(BF16)

    def b_wait(n):
        held = bbuf.at[:, parts[n]]
        pltpu.make_async_copy(held, held, b_recv.at[n]).wait()

    def b_sum(f):
        total = own[f, pl.ds(mine_own, PIECE), :]
        for d in range(CHIPS - 1):
            total = total + bbuf[d, f].astype(F32)
        return total

    b_wait(0)
    last = b_sum(FRAMES - 1).astype(BF16)
    tmsg[:PIECE, :] = last
    states[FRAMES - 1, pl.ds(mine, PIECE), :] = last

    def t_copy(d):
        return pltpu.make_async_remote_copy(
            src_ref=tmsg,
            dst_ref=tbuf.at[slab],
            send_sem=t_send.at[d],
            recv_sem=t_recv.at[slab],
            device_id={"tm": slab + d},
            device_id_type=MESH,
        )

    repeat(1, SLABS - slab, lambda d: t_copy(d).start())

    b_wait(1)
    for f in range(FRAMES - 1):
        states[f, pl.ds(mine, PIECE), :] = b_sum(f).astype(BF16)

    def c_copy(d):
        held = states.at[:, pl.ds(mine, PIECE)]
        return pltpu.make_async_remote_copy(
            src_ref=held,
            dst_ref=held,
            send_sem=c_send.at[d],
            recv_sem=c_recv,
            device_id={"lon": 2 * ((chip + d) % CHIPS) + core},
            device_id_type=MESH,
        )

    repeat(1, CHIPS, lambda d: c_copy(d).start())
    project(1, wq, q_v, False)

    first_head = (chip * PIECE) // HD
    second_head = jnp.minimum(first_head + 1, 2)
    spot = lax.broadcasted_iota(jnp.int32, (PIECE, HD), 0) + chip * PIECE
    in_first = spot < (first_head + 1) * HD

    def bring(s, total):
        pltpu.make_async_copy(tbuf.at[s], tbuf.at[s], t_recv.at[s]).wait()
        pair = tbuf[s, PIECE:, :].astype(F32)
        tdec[...] = pair[:8] + pair[8:]
        a = tdec[pl.ds(core * 3 + first_head, 1), :]
        b = tdec[pl.ds(core * 3 + second_head, 1), :]
        return jnp.where(in_first, a, b) * total + tbuf[s, :PIECE, :].astype(F32)

    total = lax.fori_loop(0, slab, bring, jnp.zeros((PIECE, HD), F32))
    inc[pl.ds(mine, PIECE), :] = total.astype(BF16)

    def i_copy(d):
        held = inc.at[pl.ds(mine, PIECE)]
        return pltpu.make_async_remote_copy(
            src_ref=held,
            dst_ref=held,
            send_sem=i_send.at[d],
            recv_sem=i_recv,
            device_id={"lon": (lon + d) % LONS},
            device_id_type=MESH,
        )

    repeat(1, LONS, lambda d: i_copy(d).start())

    held = states.at[:, pl.ds(0, OWN - PIECE)]
    pltpu.make_async_copy(held, held, c_recv).wait()
    held = states.at[:, pl.ds(pl.multiple_of(core * OWN, OWN), OWN)]
    d_copy = pltpu.make_async_remote_copy(
        src_ref=held,
        dst_ref=held,
        send_sem=d_send,
        recv_sem=d_recv,
        device_id={"lon": partner},
        device_id_type=MESH,
    )
    d_copy.start()
    held = inc.at[pl.ds(0, HK - PIECE)]
    pltpu.make_async_copy(held, held, i_recv).wait()
    d_copy.wait_recv()

    l_gain.wait()

    def read(f):
        rows = pl.ds(pl.multiple_of(f * 2 * LAT, 2 * LAT), 2 * LAT)
        alive = jnp.where(f < n_live, 1.0, 0.0).astype(F32)
        heads = []
        for h in range(HEADS):
            at = pl.ds(h * HD, HD)
            state = states[f, at, :].astype(F32) + reach[pl.ds(f * HEADS + h, 1), :] * inc[
                at, :
            ].astype(F32)
            readout = dot(q_v[:, rows, at].reshape(TOK, HD), state.astype(BF16))
            inverse = lax.rsqrt(jnp.mean(readout * readout, axis=-1, keepdims=True) + 1e-05)
            scale = gain[pl.ds(h * HD, HD)].reshape(1, HD) * alive
            heads.append((readout * inverse * scale).astype(BF16))
        back = dot(order[...], jnp.concatenate(heads, axis=1))
        normed[pl.ds(pl.multiple_of(f * TOK, TOK), TOK), :] = back.astype(BF16)

    repeat(0, FRAMES, read)
    l_wo.wait()
    out_rows = out_v.reshape(FRAMES * TOK, D)

    def out_copy(j):
        lanes = pl.ds(pl.multiple_of(j * CHUNK, CHUNK), CHUNK)
        return pltpu.make_async_copy(
            out_v.at[:, :, :, lanes], out_hbm.at[:, :, :, lanes], out_sem.at[j]
        )

    def emit(j):
        lanes = pl.ds(pl.multiple_of(j * CHUNK, CHUNK), CHUNK)
        out_rows[:, lanes] = dot(normed[...], wo[:, lanes]).astype(BF16)
        out_copy(j).start()

    repeat(0, D // CHUNK, emit)

    for copy in halos:
        copy.wait_send()
    for n in range(2):
        a_copy(n).wait_send()
        repeat(1, CHIPS, lambda d, n=n: b_copy(n, d).wait_send())
    repeat(1, SLABS - slab, lambda d: t_copy(d).wait_send())
    repeat(1, CHIPS, lambda d: c_copy(d).wait_send())
    repeat(1, LONS, lambda d: i_copy(d).wait_send())
    d_copy.wait_send()
    repeat(0, D // CHUNK, lambda j: out_copy(j).wait())


def local(frames_in, conv_kernel, w_query, w_key, w_value, w_out, norm_gain, log_gate, cam_valid, live_frames):
    dma = pltpu.SemaphoreType.DMA
    anywhere = pl.BlockSpec(memory_space=pl.ANY)
    return pl.pallas_call(
        kernel,
        out_shape=jax.ShapeDtypeStruct((FRAMES, LAT, COLS, D), BF16),
        in_specs=[anywhere] * 9 + [pl.BlockSpec(memory_space=pltpu.SMEM)],
        out_specs=anywhere,
        scratch_shapes=[
            pltpu.VMEM((FRAMES, LAT, COLS, D), BF16),
            pltpu.VMEM((3, 3, D), F32),
            pltpu.VMEM((D, HK), BF16),
            pltpu.VMEM((D, HK), BF16),
            pltpu.VMEM((D, HK), BF16),
            pltpu.VMEM((HK, D), BF16),
            pltpu.VMEM((HK,), F32),
            pltpu.VMEM((FRAMES, HEADS), F32),
            pltpu.VMEM((FRAMES, CAMS), jnp.int32),
            pltpu.VMEM((3 * TOK, TOK), BF16),
            pltpu.VMEM((3 * LAT, LAT), BF16),
            pltpu.VMEM((TOK, TOK), BF16),
            pltpu.VMEM((2, FRAMES, LAT, D), BF16),
            pltpu.VMEM((2, FRAMES, LAT, D), BF16),
            pltpu.VMEM((HALF, D), F32),
            pltpu.VMEM((2, HALF, D), BF16),
            pltpu.VMEM((2, HALF, HK), BF16),
            pltpu.VMEM((2, HALF, HK), BF16),
            pltpu.VMEM((2, HALF, HK), BF16),
            pltpu.VMEM((2, HALF, HD), F32),
            pltpu.VMEM((FRAMES * HEADS, HD), F32),
            pltpu.VMEM((FRAMES * HEADS, HD), F32),
            pltpu.VMEM((FRAMES, OWN, HD), BF16),
            pltpu.VMEM((FRAMES, OWN, HD), F32),
            pltpu.VMEM((FRAMES, OWN, HD), BF16),
            pltpu.VMEM((FRAMES, OWN, HD), BF16),
            pltpu.VMEM((CHIPS - 1, FRAMES, PIECE, HD), BF16),
            pltpu.VMEM((PIECE + 16, HD), BF16),
            pltpu.VMEM((SLABS, PIECE + 16, HD), BF16),
            pltpu.VMEM((8, HD), F32),
            pltpu.VMEM((FRAMES, HK, HD), BF16),
            pltpu.VMEM((HK, HD), BF16),
            pltpu.VMEM((FRAMES * TOK, HK), BF16),
            pltpu.VMEM((FRAMES, LAT, COLS, D), BF16),
            dma((9,)),
            dma((D // CHUNK,)),
            dma((2,)),
            dma((2,)),
            dma((2,)),
            dma((2,)),
            dma((2, CHIPS)),
            dma((2,)),
            dma((SLABS,)),
            dma((SLABS,)),
            dma((CHIPS,)),
            dma,
            dma,
            dma,
            dma((LONS,)),
            dma,
        ],
        compiler_params=pltpu.CompilerParams(
            collective_id=0, has_side_effects=True, vmem_limit_bytes=56 * 1024 * 1024
        ),
    )(frames_in, conv_kernel, w_query, w_key, w_value, w_out, norm_gain, log_gate, cam_valid, live_frames)


def solution(mesh):
    in_specs = (
        P("tm", None, "lon", None),
        P(),
        P(),
        P(),
        P(),
        P(),
        P(),
        P("tm", None),
        P("tm", None),
        P("tm"),
    )
    out_specs = P("tm", None, "lon", None)
    return jax.shard_map(local, mesh=mesh, in_specs=in_specs, out_specs=out_specs, check_vma=False)
```

```python
import jax
import jax.numpy as jnp
from jax import lax
from jax.experimental import pallas as pl
from jax.experimental.pallas import tpu as pltpu
from jax.sharding import PartitionSpec as P

MESH = pl.DeviceIdType.MESH
F32 = jnp.float32
BF16 = jnp.bfloat16

HEADS = 6
HD = 128
CAMS = 6
FRAMES = 4
LAT = 32
COLS = 4
D = 1536
HK = HEADS * HD
TOK = LAT * COLS
LONG = 64
CHUNK = 256
HALF = FRAMES * 2 * LAT
OWN = HK // 2
CHIPS = 8
PIECE = OWN // CHIPS
PARTS = ((0, 1), (3,), (2,))
SLABS = 16
LONS = 16


def repeat(first, last, body, unroll=1):
    def step(i, carry):
        body(i)
        return carry

    lax.fori_loop(first, last, step, 0, unroll=unroll)


def dot(a, b):
    return jnp.dot(a, b, preferred_element_type=F32)


def column_of(t):
    block = t // LAT
    return jnp.where(block == 0, 1, jnp.where(block == 1, 2, jnp.where(block == 2, 0, 3)))


def kernel(
    x_hbm,
    ck_hbm,
    wq_hbm,
    wk_hbm,
    wv_hbm,
    gain_hbm,
    lg_hbm,
    cam_hbm,
    live_hbm,
    normed,
    live_ref,
    x_v,
    ck,
    wq,
    wk,
    wv,
    gain,
    lg,
    cam,
    shift3,
    shift_h,
    order,
    edge_out,
    edge_in,
    partial,
    mixed,
    q_v,
    k_v,
    v_v,
    keep,
    dec,
    reach,
    other,
    other_sum,
    own,
    own_sum,
    abuf,
    bsend,
    bbuf,
    tbuf,
    dsend,
    tdec,
    states,
    inc,
    load_sem,
    halo_send,
    halo_recv,
    a_send,
    a_recv,
    b_send,
    b_recv,
    dec_send,
    dec_recv,
    t_send,
    t_recv,
    c_send,
    c_recv,
    d_send,
    d_recv,
    i_send,
    i_recv,
    e_send,
    e_recv,
):
    lon = lax.axis_index("lon")
    slab = lax.axis_index("tm")
    core = lon % 2
    chip = lon // 2
    partner = lon + 1 - 2 * core
    half = pl.multiple_of(core * OWN, OWN)
    mine_own = pl.multiple_of(chip * PIECE, 16)
    mine = pl.multiple_of(core * OWN + chip * PIECE, 16)

    loads = []
    for n, (src, dst) in enumerate(
        (
            (x_hbm, x_v),
            (live_hbm, live_ref),
            (ck_hbm, ck),
            (lg_hbm, lg),
            (cam_hbm, cam),
            (gain_hbm, gain),
            (wk_hbm, wk),
            (wv_hbm, wv),
            (wq_hbm, wq),
        )
    ):
        copy = pltpu.make_async_copy(src, dst, load_sem.at[n])
        copy.start()
        loads.append(copy)
    l_x, l_live, l_ck, l_lg, l_cam, l_gain, l_wk, l_wv, l_wq = loads

    barrier = pltpu.get_barrier_semaphore()

    def greet(d):
        pl.semaphore_signal(
            barrier, inc=1, device_id={"lon": (lon + d) % LONS}, device_id_type=MESH
        )
        pl.semaphore_signal(
            barrier, inc=1, device_id={"tm": (slab + d) % SLABS}, device_id_type=MESH
        )

    repeat(1, LONS, greet)

    def to_lon(src, dst, send, recv, target):
        return pltpu.make_async_remote_copy(
            src_ref=src,
            dst_ref=dst,
            send_sem=send,
            recv_sem=recv,
            device_id={"lon": target},
            device_id_type=MESH,
        )

    def wait_for(held, sem):
        pltpu.make_async_copy(held, held, sem).wait()

    row = lax.broadcasted_iota(jnp.int32, (TOK, TOK), 0)
    col = lax.broadcasted_iota(jnp.int32, (TOK, TOK), 1)
    c_row = column_of(row)
    for i in range(3):
        lat = row % LAT + (i - 1)
        hit = (lat >= 0) & (lat < LAT) & (col == lat * COLS + c_row)
        shift3[i * TOK : (i + 1) * TOK, :] = jnp.where(hit, 1.0, 0.0).astype(BF16)
    hit = row == (col % LAT) * COLS + column_of(col)
    order[...] = jnp.where(hit, 1.0, 0.0).astype(BF16)
    row = lax.broadcasted_iota(jnp.int32, (3 * LAT, LAT), 0)
    col = lax.broadcasted_iota(jnp.int32, (3 * LAT, LAT), 1)
    shift_h[...] = jnp.where(col == row % LAT + row // LAT - 1, 1.0, 0.0).astype(BF16)

    l_x.wait()
    x_rows = x_v.reshape(FRAMES * TOK, D)
    for f in range(FRAMES):

        def extract(j):
            lanes = pl.ds(pl.multiple_of(j * CHUNK, CHUNK), CHUNK)
            planes = dot(shift3[TOK + 2 * LAT : 2 * TOK, :], x_rows[f * TOK : (f + 1) * TOK, lanes])
            planes = planes.astype(BF16)
            edge_out[1, f, :, lanes] = planes[:LAT]
            edge_out[0, f, :, lanes] = planes[LAT:]

        repeat(0, D // CHUNK, extract, 3)

    def halo_copy(side, f):
        target = (lon + (1 if side == 0 else LONS - 1)) % LONS
        return to_lon(
            edge_out.at[side, f],
            edge_in.at[side, f],
            halo_send.at[side, f],
            halo_recv.at[side, f],
            target,
        )

    pl.semaphore_wait(barrier, 2 * (LONS - 1))
    for f in range(FRAMES):
        for side in range(2):
            halo_copy(side, f).start()

    l_live.wait()
    l_lg.wait()
    l_cam.wait()
    n_live = live_ref[0]
    frame = lax.broadcasted_iota(jnp.int32, (FRAMES, HEADS), 0)
    live = jnp.where(frame < n_live, 1.0, 0.0).astype(F32)
    decay = jnp.exp(lg[...] * live)
    sofar = decay[0:1]
    for f in range(FRAMES):
        if f:
            sofar = sofar * decay[f : f + 1]
        for h in range(HEADS):
            at = f * HEADS + h
            dec[at : at + 1, :] = jnp.broadcast_to(decay[f : f + 1, h : h + 1], (1, HD))
            reach[at : at + 1, :] = jnp.broadcast_to(sofar[:, h : h + 1], (1, HD))
    dsend[...] = jnp.concatenate(
        [reach[(FRAMES - 1) * HEADS :, :], jnp.zeros((8 - HEADS, HD), F32)], axis=0
    )

    def dec_copy(d):
        return pltpu.make_async_remote_copy(
            src_ref=dsend,
            dst_ref=tdec.at[slab],
            send_sem=dec_send.at[d],
            recv_sem=dec_recv.at[slab],
            device_id={"tm": slab + d},
            device_id_type=MESH,
        )

    repeat(1, SLABS - slab, lambda d: dec_copy(d).start())
    valid = cam[...].astype(F32) * live
    lane = lax.broadcasted_iota(jnp.int32, (1, CAMS), 1)
    for n, c in enumerate((1, 2, 0, 3)):
        camera = ((lon * COLS + c) * CAMS) // LONG
        for f in range(FRAMES):
            bit = jnp.sum(jnp.where(lane == camera, valid[f : f + 1], 0.0), axis=1, keepdims=True)
            at = f * 2 * LAT + (n % 2) * LAT
            keep[n // 2, at : at + LAT, :] = jnp.broadcast_to(bit, (LAT, HD))

    l_ck.wait()

    def taps(j):
        lanes = pl.ds(pl.multiple_of(j * CHUNK, CHUNK), CHUNK)
        k = [[0.5 * ck[i, n : n + 1, lanes] for n in range(3)] for i in range(3)]

        def one(f):
            x = x_rows[pl.ds(pl.multiple_of(f * TOK, TOK), TOK), lanes]
            s = [dot(shift3[i * TOK : (i + 1) * TOK, :], x) for i in range(3)]
            place = {1: 0, 2: 1, 0: 2, 3: 3}

            def plane(i, c):
                at = place[c] * LAT
                return s[i][at : at + LAT]

            at = pl.multiple_of(f * 2 * LAT, 2 * LAT)
            for n, c in enumerate((1, 2, 0, 3)):
                total = None
                for i in range(3):
                    for m in range(3):
                        if 0 <= c + m - 1 < COLS:
                            term = k[i][m] * plane(i, c + m - 1)
                            total = term if total is None else total + term
                rows = pl.ds(at + (n % 2) * LAT, LAT)
                if n < 2:
                    mixed[0, rows, lanes] = (total * jnp.tanh(total) + total).astype(BF16)
                else:
                    partial[rows, lanes] = total

        repeat(0, FRAMES, one, FRAMES)

    repeat(0, D // CHUNK, taps)

    def project(side, first, count, weights, dst, masked, unroll):
        rows = pl.ds(first, count)

        def one(j):
            lanes = pl.ds(pl.multiple_of(j * CHUNK, CHUNK), CHUNK)
            r = dot(mixed[side, rows, :], weights[:, lanes])
            if masked:
                m = keep[side, rows, :]
                r = r * jnp.concatenate([m, m], axis=1)
            dst[side, rows, lanes] = r.astype(BF16)

        repeat(0, HK // CHUNK, one, unroll)

    l_wk.wait()
    project(0, 0, HALF, wk, k_v, True, 3)
    l_wv.wait()
    project(0, 0, HALF, wv, v_v, False, 3)

    l_wq.wait()
    project(0, 0, HALF, wq, q_v, False, 3)

    def edge_taps(f):
        def one(j):
            lanes = pl.ds(pl.multiple_of(j * CHUNK, CHUNK), CHUNK)
            for side in range(2):
                s = dot(shift_h[...], edge_in[side, f, :, lanes])
                rows = pl.ds(f * 2 * LAT + side * LAT, LAT)
                total = partial[rows, lanes]
                for i in range(3):
                    tap = 0.5 * ck[i, 2 * side : 2 * side + 1, lanes]
                    total = total + tap * s[i * LAT : (i + 1) * LAT]
                mixed[1, rows, lanes] = (total * jnp.tanh(total) + total).astype(BF16)

        repeat(0, D // CHUNK, one, D // CHUNK)

    def scan_heads(frames, first, carried, put):
        def one(n):
            h = first + n
            lanes = pl.ds(pl.multiple_of(h * HD, HD), HD)
            at = pl.ds(pl.multiple_of(n * HD, HD), HD)
            total = None
            for f in frames:
                rows = pl.ds(f * 2 * LAT, 2 * LAT)
                keys = k_v[:, rows, lanes].reshape(TOK, HD)
                values = v_v[:, rows, lanes].reshape(TOK, HD)
                term = lax.dot_general(
                    keys, values, (((0,), (0,)), ((), ())), preferred_element_type=F32
                )
                if f:
                    before = carried[at, :] if total is None else total
                    term = term + dec[pl.ds(f * HEADS + h, 1), :] * before
                total = term
                put(f, at, total)
            carried[at, :] = total

        repeat(0, 3, one, 3)

    def put_other(f, at, total):
        other[f, at, :] = total.astype(BF16)

    def put_own(f, at, total):
        own[f, at, :] = total

    def frames_of(p):
        return pl.ds(PARTS[p][0], len(PARTS[p]))

    def a_copy(p):
        at = frames_of(p)
        return to_lon(other.at[at], abuf.at[at], a_send.at[p], a_recv.at[p], partner)

    def b_copy(p, d):
        to = (chip + d) % CHIPS
        rows = pl.ds(pl.multiple_of(to * PIECE, 16), PIECE)
        return to_lon(
            bsend.at[frames_of(p), rows],
            bbuf.at[d - 1, frames_of(p)],
            b_send.at[p, d],
            b_recv.at[p],
            2 * to + core,
        )

    def c_copy(p, d):
        held = states.at[frames_of(p), pl.ds(mine, PIECE)]
        to = (chip + d) % CHIPS
        return to_lon(held, held, c_send.at[p, d], c_recv.at[p], 2 * to + core)

    def d_copy(p):
        held = states.at[frames_of(p), pl.ds(half, OWN)]
        return to_lon(held, held, d_send.at[p], d_recv.at[p], partner)

    def t_copy(d):
        return pltpu.make_async_remote_copy(
            src_ref=states.at[FRAMES - 1, pl.ds(mine, PIECE)],
            dst_ref=tbuf.at[slab],
            send_sem=t_send.at[d],
            recv_sem=t_recv.at[slab],
            device_id={"tm": slab + d},
            device_id_type=MESH,
        )

    def after_a(p):
        a_copy(p).wait_recv()
        for f in PARTS[p]:
            for n in range(3):
                rows = pl.ds(n * HD, HD)
                total = own[f, rows, :] + abuf[f, rows, :].astype(F32)
                own[f, rows, :] = total
                bsend[f, rows, :] = total.astype(BF16)
        repeat(1, CHIPS, lambda d: b_copy(p, d).start())

    def after_b(p):
        wait_for(bbuf.at[:, frames_of(p)], b_recv.at[p])
        for f in PARTS[p]:
            total = own[f, pl.ds(mine_own, PIECE), :]
            for d in range(CHIPS - 1):
                total = total + bbuf[d, f].astype(F32)
            states[f, pl.ds(mine, PIECE), :] = total.astype(BF16)
        if PARTS[p][0] == FRAMES - 1:
            repeat(1, SLABS - slab, lambda d: t_copy(d).start())
        repeat(1, CHIPS, lambda d: c_copy(p, d).start())

    def after_c(p):
        wait_for(states.at[frames_of(p), pl.ds(0, OWN - PIECE)], c_recv.at[p])
        d_copy(p).start()

    for group in ((0, 1), (2, 3)):
        for f in group:
            for side in range(2):
                halo_copy(side, f).wait_recv()
            edge_taps(f)
        first = group[0] * 2 * LAT
        if first:
            after_a(0)
        project(1, first, 4 * LAT, wk, k_v, True, 3)
        project(1, first, 4 * LAT, wv, v_v, False, 3)
        scan_heads(group, (1 - core) * 3, other_sum, put_other)
        if first:
            a_copy(1).start()
            a_copy(2).start()
        else:
            a_copy(0).start()
        scan_heads(group, core * 3, own_sum, put_own)
    after_a(1)
    after_a(2)
    after_b(0)
    after_b(1)
    after_b(2)
    project(1, 0, HALF, wq, q_v, False, 3)
    after_c(0)

    first_head = mine_own // HD
    second_head = jnp.minimum(first_head + 1, 2)
    spot = lax.broadcasted_iota(jnp.int32, (PIECE, HD), 0) + mine_own
    in_first = spot < (first_head + 1) * HD

    def bring(s, total):
        wait_for(tdec.at[s], dec_recv.at[s])
        wait_for(tbuf.at[s], t_recv.at[s])
        a = tdec[s, pl.ds(core * 3 + first_head, 1), :]
        b = tdec[s, pl.ds(core * 3 + second_head, 1), :]
        return jnp.where(in_first, a, b) * total + tbuf[s].astype(F32)

    total = lax.fori_loop(0, slab, bring, jnp.zeros((PIECE, HD), F32))
    inc[pl.ds(mine, PIECE), :] = total.astype(BF16)

    def i_copy(d):
        held = inc.at[pl.ds(mine, PIECE)]
        return to_lon(held, held, i_send.at[d], i_recv, (lon + 2 * d) % LONS)

    repeat(1, LONS // 2, lambda d: i_copy(d).start())
    after_c(1)
    after_c(2)
    wait_for(inc.at[pl.ds(0, OWN - PIECE)], i_recv)
    held = inc.at[pl.ds(half, OWN)]
    e_copy = to_lon(held, held, e_send, e_recv, partner)
    e_copy.start()
    for p in range(3):
        d_copy(p).wait_recv()
    e_copy.wait_recv()

    l_gain.wait()

    def read(f):
        rows = pl.ds(pl.multiple_of(f * 2 * LAT, 2 * LAT), 2 * LAT)
        alive = jnp.where(f < n_live, 1.0, 0.0).astype(F32)
        heads = []
        for h in range(HEADS):
            at = pl.ds(h * HD, HD)
            state = states[f, at, :].astype(F32) + reach[pl.ds(f * HEADS + h, 1), :] * inc[
                at, :
            ].astype(F32)
            readout = dot(q_v[:, rows, at].reshape(TOK, HD), state.astype(BF16))
            inverse = lax.rsqrt(jnp.mean(readout * readout, axis=-1, keepdims=True) + 1e-05)
            scale = gain[pl.ds(h * HD, HD)].reshape(1, HD) * alive
            heads.append((readout * inverse * scale).astype(BF16))
        back = dot(order[...], jnp.concatenate(heads, axis=1))
        normed[pl.ds(pl.multiple_of(f * TOK, TOK), TOK), :] = back.astype(BF16)

    repeat(0, FRAMES, read, FRAMES)

    for f in range(FRAMES):
        for side in range(2):
            halo_copy(side, f).wait_send()
    for p in range(3):
        a_copy(p).wait_send()
        repeat(1, CHIPS, lambda d, p=p: b_copy(p, d).wait_send())
        repeat(1, CHIPS, lambda d, p=p: c_copy(p, d).wait_send())
        d_copy(p).wait_send()
    repeat(1, SLABS - slab, lambda d: dec_copy(d).wait_send())
    repeat(1, SLABS - slab, lambda d: t_copy(d).wait_send())
    repeat(1, LONS // 2, lambda d: i_copy(d).wait_send())
    e_copy.wait_send()


def out_kernel(normed, wo, out_hbm, out_v, out_sem):
    out_rows = out_v.reshape(FRAMES * TOK, D)

    def out_copy(j):
        lanes = pl.ds(pl.multiple_of(j * CHUNK, CHUNK), CHUNK)
        return pltpu.make_async_copy(
            out_v.at[:, :, :, lanes], out_hbm.at[:, :, :, lanes], out_sem.at[j]
        )

    def emit(j):
        lanes = pl.ds(pl.multiple_of(j * CHUNK, CHUNK), CHUNK)
        out_rows[:, lanes] = dot(normed[...], wo[:, lanes]).astype(BF16)
        out_copy(j).start()

    repeat(0, D // CHUNK, emit, 2)
    repeat(0, D // CHUNK, lambda j: out_copy(j).wait())


def local(frames_in, conv_kernel, w_query, w_key, w_value, w_out, norm_gain, log_gate, cam_valid, live_frames):
    dma = pltpu.SemaphoreType.DMA
    anywhere = pl.BlockSpec(memory_space=pltpu.HBM)
    held = pl.BlockSpec(memory_space=pltpu.VMEM)
    normed = pl.pallas_call(
        kernel,
        out_shape=jax.ShapeDtypeStruct((FRAMES * TOK, HK), BF16),
        in_specs=[anywhere] * 9,
        out_specs=held,
        scratch_shapes=[
            pltpu.SMEM((1,), jnp.int32),
            pltpu.VMEM((FRAMES, LAT, COLS, D), BF16),
            pltpu.VMEM((3, 3, D), F32),
            pltpu.VMEM((D, HK), BF16),
            pltpu.VMEM((D, HK), BF16),
            pltpu.VMEM((D, HK), BF16),
            pltpu.VMEM((HK,), F32),
            pltpu.VMEM((FRAMES, HEADS), F32),
            pltpu.VMEM((FRAMES, CAMS), jnp.int32),
            pltpu.VMEM((3 * TOK, TOK), BF16),
            pltpu.VMEM((3 * LAT, LAT), BF16),
            pltpu.VMEM((TOK, TOK), BF16),
            pltpu.VMEM((2, FRAMES, LAT, D), BF16),
            pltpu.VMEM((2, FRAMES, LAT, D), BF16),
            pltpu.VMEM((HALF, D), F32),
            pltpu.VMEM((2, HALF, D), BF16),
            pltpu.VMEM((2, HALF, HK), BF16),
            pltpu.VMEM((2, HALF, HK), BF16),
            pltpu.VMEM((2, HALF, HK), BF16),
            pltpu.VMEM((2, HALF, HD), F32),
            pltpu.VMEM((FRAMES * HEADS, HD), F32),
            pltpu.VMEM((FRAMES * HEADS, HD), F32),
            pltpu.VMEM((FRAMES, OWN, HD), BF16),
            pltpu.VMEM((OWN, HD), F32),
            pltpu.VMEM((FRAMES, OWN, HD), F32),
            pltpu.VMEM((OWN, HD), F32),
            pltpu.VMEM((FRAMES, OWN, HD), BF16),
            pltpu.VMEM((FRAMES, OWN, HD), BF16),
            pltpu.VMEM((CHIPS - 1, FRAMES, PIECE, HD), BF16),
            pltpu.VMEM((SLABS, PIECE, HD), BF16),
            pltpu.VMEM((8, HD), F32),
            pltpu.VMEM((SLABS, 8, HD), F32),
            pltpu.VMEM((FRAMES, HK, HD), BF16),
            pltpu.VMEM((HK, HD), BF16),
            dma((9,)),
            dma((2, FRAMES)),
            dma((2, FRAMES)),
            dma((3,)),
            dma((3,)),
            dma((3, CHIPS)),
            dma((3,)),
            dma((SLABS,)),
            dma((SLABS,)),
            dma((SLABS,)),
            dma((SLABS,)),
            dma((3, CHIPS)),
            dma((3,)),
            dma((3,)),
            dma((3,)),
            dma((LONS // 2,)),
            dma,
            dma,
            dma,
        ],
        compiler_params=pltpu.CompilerParams(
            collective_id=0, has_side_effects=True, vmem_limit_bytes=58 * 1024 * 1024
        ),
    )(frames_in, conv_kernel, w_query, w_key, w_value, norm_gain, log_gate, cam_valid, live_frames)
    return pl.pallas_call(
        out_kernel,
        out_shape=jax.ShapeDtypeStruct((FRAMES, LAT, COLS, D), BF16),
        in_specs=[held, held],
        out_specs=anywhere,
        scratch_shapes=[
            pltpu.VMEM((FRAMES, LAT, COLS, D), BF16),
            dma((D // CHUNK,)),
        ],
        compiler_params=pltpu.CompilerParams(vmem_limit_bytes=16 * 1024 * 1024),
    )(normed, w_out)


def solution(mesh):
    in_specs = (
        P("tm", None, "lon", None),
        P(),
        P(),
        P(),
        P(),
        P(),
        P(),
        P("tm", None),
        P("tm", None),
        P("tm"),
    )
    out_specs = P("tm", None, "lon", None)
    return jax.shard_map(local, mesh=mesh, in_specs=in_specs, out_specs=out_specs, check_vma=False)
```

```python
import jax
import jax.numpy as jnp
from jax import lax
from jax.experimental import pallas as pl
from jax.experimental.pallas import tpu as pltpu
from jax.sharding import PartitionSpec as P

MESH = pl.DeviceIdType.MESH
F32 = jnp.float32
BF16 = jnp.bfloat16

HEADS = 6
HD = 128
CAMS = 6
FRAMES = 4
LAT = 32
COLS = 4
D = 1536
HK = HEADS * HD
TOK = LAT * COLS
LONG = 64
CHUNK = 256
HALF = FRAMES * 2 * LAT
OWN = HK // 2
CHIPS = 8
PIECE = OWN // CHIPS
PARTS = ((0, 1), (3,), (2,))
SLABS = 16
LONS = 16


def repeat(first, last, body, unroll=1):
    def step(i, carry):
        body(i)
        return carry

    lax.fori_loop(first, last, step, 0, unroll=unroll)


def dot(a, b):
    return jnp.dot(a, b, preferred_element_type=F32)


def column_of(t):
    block = t // LAT
    return jnp.where(block == 0, 1, jnp.where(block == 1, 2, jnp.where(block == 2, 0, 3)))


def kernel(
    x_hbm,
    ck_hbm,
    wq_hbm,
    wk_hbm,
    wv_hbm,
    wo_hbm,
    gain_hbm,
    lg_hbm,
    cam_hbm,
    live_hbm,
    out_hbm,
    live_ref,
    x_v,
    ck,
    wq,
    wk,
    wv,
    wo,
    gain,
    lg,
    cam,
    shift3,
    shift_h,
    order,
    edge_out,
    edge_in,
    partial,
    mixed,
    q_v,
    k_v,
    v_v,
    keep,
    dec,
    reach,
    other,
    other_sum,
    own,
    own_sum,
    abuf,
    bsend,
    bbuf,
    tbuf,
    dsend,
    tdec,
    weight,
    states,
    inc,
    normed,
    out_v,
    load_sem,
    out_sem,

    halo_send,
    halo_recv,
    a_send,
    a_recv,
    b_send,
    b_recv,
    dec_send,
    dec_recv,
    t_send,
    t_recv,
    c_send,
    c_recv,
    d_send,
    d_recv,
    i_send,
    i_recv,
    e_send,
    e_recv,
):
    lon = lax.axis_index("lon")
    slab = lax.axis_index("tm")
    core = lon % 2
    chip = lon // 2
    partner = lon + 1 - 2 * core
    half = pl.multiple_of(core * OWN, OWN)
    mine_own = pl.multiple_of(chip * PIECE, 16)
    mine = pl.multiple_of(core * OWN + chip * PIECE, 16)

    loads = []
    for n, (src, dst) in enumerate(
        (
            (x_hbm.at[0], x_v.at[0]),
            (live_hbm, live_ref),
            (lg_hbm, lg),
            (cam_hbm, cam),
            (x_hbm.at[1], x_v.at[1]),
            (x_hbm.at[2], x_v.at[2]),
            (x_hbm.at[3], x_v.at[3]),
            (ck_hbm, ck),
            (gain_hbm, gain),
            (wk_hbm, wk),
            (wv_hbm, wv),
            (wq_hbm, wq),
            (wo_hbm, wo),
        )
    ):
        copy = pltpu.make_async_copy(src, dst, load_sem.at[n])
        copy.start()
        loads.append(copy)
    l_x0, l_live, l_lg, l_cam, l_x1, l_x2, l_x3, l_ck, l_gain, l_wk, l_wv, l_wq, l_wo = loads
    l_x = (l_x0, l_x1, l_x2, l_x3)

    barrier = pltpu.get_barrier_semaphore()

    def greet(d):
        pl.semaphore_signal(
            barrier, inc=1, device_id={"lon": (lon + d) % LONS}, device_id_type=MESH
        )
        pl.semaphore_signal(
            barrier, inc=1, device_id={"tm": (slab + d) % SLABS}, device_id_type=MESH
        )

    repeat(1, LONS, greet)

    def to_lon(src, dst, send, recv, target):
        return pltpu.make_async_remote_copy(
            src_ref=src,
            dst_ref=dst,
            send_sem=send,
            recv_sem=recv,
            device_id={"lon": target},
            device_id_type=MESH,
        )

    def wait_for(held, sem):
        pltpu.make_async_copy(held, held, sem).wait()

    row = lax.broadcasted_iota(jnp.int32, (TOK, TOK), 0)
    col = lax.broadcasted_iota(jnp.int32, (TOK, TOK), 1)
    c_row = column_of(row)
    for i in range(3):
        lat = row % LAT + (i - 1)
        hit = (lat >= 0) & (lat < LAT) & (col == lat * COLS + c_row)
        shift3[i * TOK : (i + 1) * TOK, :] = jnp.where(hit, 1.0, 0.0).astype(BF16)
    hit = row == (col % LAT) * COLS + column_of(col)
    order[...] = jnp.where(hit, 1.0, 0.0).astype(BF16)
    row = lax.broadcasted_iota(jnp.int32, (3 * LAT, LAT), 0)
    col = lax.broadcasted_iota(jnp.int32, (3 * LAT, LAT), 1)
    shift_h[...] = jnp.where(col == row % LAT + row // LAT - 1, 1.0, 0.0).astype(BF16)

    l_live.wait()
    l_lg.wait()
    l_cam.wait()
    n_live = live_ref[0]
    frame = lax.broadcasted_iota(jnp.int32, (FRAMES, HEADS), 0)
    live = jnp.where(frame < n_live, 1.0, 0.0).astype(F32)
    decay = jnp.exp(lg[...] * live)
    sofar = decay[0:1]
    for f in range(FRAMES):
        if f:
            sofar = sofar * decay[f : f + 1]
        for h in range(HEADS):
            at = f * HEADS + h
            dec[at : at + 1, :] = jnp.broadcast_to(decay[f : f + 1, h : h + 1], (1, HD))
            reach[at : at + 1, :] = jnp.broadcast_to(sofar[:, h : h + 1], (1, HD))
    dsend[...] = jnp.concatenate(
        [reach[(FRAMES - 1) * HEADS :, :], jnp.zeros((8 - HEADS, HD), F32)], axis=0
    )

    valid = cam[...].astype(F32) * live
    lane = lax.broadcasted_iota(jnp.int32, (1, CAMS), 1)
    for n, c in enumerate((1, 2, 0, 3)):
        camera = ((lon * COLS + c) * CAMS) // LONG
        for f in range(FRAMES):
            bit = jnp.sum(jnp.where(lane == camera, valid[f : f + 1], 0.0), axis=1, keepdims=True)
            at = f * 2 * LAT + (n % 2) * LAT
            keep[n // 2, at : at + LAT, :] = jnp.broadcast_to(bit, (LAT, HD))

    def dec_copy(d):
        return pltpu.make_async_remote_copy(
            src_ref=dsend,
            dst_ref=tdec.at[slab],
            send_sem=dec_send.at[d],
            recv_sem=dec_recv.at[slab],
            device_id={"tm": slab + d},
            device_id_type=MESH,
        )

    x_rows = x_v.reshape(FRAMES * TOK, D)

    def halo_copy(side, f):
        target = (lon + (1 if side == 0 else LONS - 1)) % LONS
        return to_lon(
            edge_out.at[side, f],
            edge_in.at[side, f],
            halo_send.at[side, f],
            halo_recv.at[side, f],
            target,
        )

    for f in range(FRAMES):
        l_x[f].wait()

        def extract(j, f=f):
            lanes = pl.ds(pl.multiple_of(j * CHUNK, CHUNK), CHUNK)
            planes = dot(shift3[TOK + 2 * LAT : 2 * TOK, :], x_rows[f * TOK : (f + 1) * TOK, lanes])
            planes = planes.astype(BF16)
            edge_out[1, f, :, lanes] = planes[:LAT]
            edge_out[0, f, :, lanes] = planes[LAT:]

        repeat(0, D // CHUNK, extract, 6)
        if f == 0:
            pl.semaphore_wait(barrier, 2 * (LONS - 1))
        for side in range(2):
            halo_copy(side, f).start()
    repeat(1, SLABS - slab, lambda d: dec_copy(d).start())

    l_ck.wait()

    def taps(j):
        lanes = pl.ds(pl.multiple_of(j * CHUNK, CHUNK), CHUNK)
        k = [[0.5 * ck[i, n : n + 1, lanes] for n in range(3)] for i in range(3)]

        def one(f):
            x = x_rows[pl.ds(pl.multiple_of(f * TOK, TOK), TOK), lanes]
            s = [dot(shift3[i * TOK : (i + 1) * TOK, :], x) for i in range(3)]
            place = {1: 0, 2: 1, 0: 2, 3: 3}

            def plane(i, c):
                at = place[c] * LAT
                return s[i][at : at + LAT]

            at = pl.multiple_of(f * 2 * LAT, 2 * LAT)
            for n, c in enumerate((1, 2, 0, 3)):
                total = None
                for i in range(3):
                    for m in range(3):
                        if 0 <= c + m - 1 < COLS:
                            term = k[i][m] * plane(i, c + m - 1)
                            total = term if total is None else total + term
                rows = pl.ds(at + (n % 2) * LAT, LAT)
                if n < 2:
                    mixed[0, rows, lanes] = (total * jnp.tanh(total) + total).astype(BF16)
                else:
                    partial[rows, lanes] = total

        repeat(0, FRAMES, one, FRAMES)

    repeat(0, D // CHUNK, taps, 2)

    def project(side, first, count, weights, dst, masked, unroll):
        rows = pl.ds(first, count)

        def one(j):
            lanes = pl.ds(pl.multiple_of(j * CHUNK, CHUNK), CHUNK)
            r = dot(mixed[side, rows, :], weights[:, lanes])
            if masked:
                m = keep[side, rows, :]
                r = r * jnp.concatenate([m, m], axis=1)
            dst[side, rows, lanes] = r.astype(BF16)

        repeat(0, HK // CHUNK, one, unroll)

    l_wk.wait()
    project(0, 0, HALF, wk, k_v, True, 3)
    l_wv.wait()
    project(0, 0, HALF, wv, v_v, False, 3)

    def edge_taps(f):
        def one(j):
            lanes = pl.ds(pl.multiple_of(j * CHUNK, CHUNK), CHUNK)
            for side in range(2):
                s = dot(shift_h[...], edge_in[side, f, :, lanes])
                rows = pl.ds(f * 2 * LAT + side * LAT, LAT)
                total = partial[rows, lanes]
                for i in range(3):
                    tap = 0.5 * ck[i, 2 * side : 2 * side + 1, lanes]
                    total = total + tap * s[i * LAT : (i + 1) * LAT]
                mixed[1, rows, lanes] = (total * jnp.tanh(total) + total).astype(BF16)

        repeat(0, D // CHUNK, one, D // CHUNK)

    def scan_heads(frames, first, carried, put):
        def one(n):
            h = first + n
            lanes = pl.ds(pl.multiple_of(h * HD, HD), HD)
            at = pl.ds(pl.multiple_of(n * HD, HD), HD)
            total = None
            for f in frames:
                rows = pl.ds(f * 2 * LAT, 2 * LAT)
                keys = k_v[:, rows, lanes].reshape(TOK, HD)
                values = v_v[:, rows, lanes].reshape(TOK, HD)
                term = lax.dot_general(
                    keys, values, (((0,), (0,)), ((), ())), preferred_element_type=F32
                )
                if f:
                    before = carried[at, :] if total is None else total
                    term = term + dec[pl.ds(f * HEADS + h, 1), :] * before
                total = term
                put(f, at, total)
            carried[at, :] = total

        repeat(0, 3, one, 3)

    def put_other(f, at, total):
        other[f, at, :] = total.astype(BF16)

    def put_own(f, at, total):
        own[f, at, :] = total

    def frames_of(p):
        return pl.ds(PARTS[p][0], len(PARTS[p]))

    def a_copy(p):
        at = frames_of(p)
        return to_lon(other.at[at], abuf.at[at], a_send.at[p], a_recv.at[p], partner)

    def b_copy(p, d):
        to = (chip + d) % CHIPS
        rows = pl.ds(pl.multiple_of(to * PIECE, 16), PIECE)
        return to_lon(
            bsend.at[frames_of(p), rows],
            bbuf.at[d - 1, frames_of(p)],
            b_send.at[p, d],
            b_recv.at[p],
            2 * to + core,
        )

    def c_copy(p, d):
        held = states.at[frames_of(p), pl.ds(mine, PIECE)]
        to = (chip + d) % CHIPS
        return to_lon(held, held, c_send.at[p, d], c_recv.at[p], 2 * to + core)

    def d_copy(p):
        held = states.at[frames_of(p), pl.ds(half, OWN)]
        return to_lon(held, held, d_send.at[p], d_recv.at[p], partner)

    def t_copy(d):
        return pltpu.make_async_remote_copy(
            src_ref=states.at[FRAMES - 1, pl.ds(mine, PIECE)],
            dst_ref=tbuf.at[slab],
            send_sem=t_send.at[d],
            recv_sem=t_recv.at[slab],
            device_id={"tm": slab + d},
            device_id_type=MESH,
        )

    def after_a(p):
        a_copy(p).wait_recv()
        for f in PARTS[p]:
            for n in range(3):
                rows = pl.ds(n * HD, HD)
                total = own[f, rows, :] + abuf[f, rows, :].astype(F32)
                own[f, rows, :] = total
                bsend[f, rows, :] = total.astype(BF16)
        repeat(1, CHIPS, lambda d: b_copy(p, d).start())

    def after_b(p):
        wait_for(bbuf.at[:, frames_of(p)], b_recv.at[p])
        for f in PARTS[p]:
            total = own[f, pl.ds(mine_own, PIECE), :]
            for d in range(CHIPS - 1):
                total = total + bbuf[d, f].astype(F32)
            states[f, pl.ds(mine, PIECE), :] = total.astype(BF16)

    def send_c(p):
        repeat(1, CHIPS, lambda d: c_copy(p, d).start())

    def after_c(p):
        wait_for(states.at[frames_of(p), pl.ds(0, OWN - PIECE)], c_recv.at[p])
        d_copy(p).start()

    for group in ((0, 1), (2, 3)):
        for f in group:
            for side in range(2):
                halo_copy(side, f).wait_recv()
            edge_taps(f)
        first = group[0] * 2 * LAT
        if first:
            after_a(0)
        project(1, first, 4 * LAT, wk, k_v, True, 3)
        project(1, first, 4 * LAT, wv, v_v, False, 3)
        scan_heads(group, (1 - core) * 3, other_sum, put_other)
        if first:
            a_copy(1).start()
            a_copy(2).start()
        else:
            a_copy(0).start()
        scan_heads(group, core * 3, own_sum, put_own)
    after_a(1)
    after_a(2)
    after_b(0)
    send_c(0)
    after_b(1)
    for d in (4, 12, 5, 3, 11, 13, 2, 6, 10, 14, 8, 1, 7, 9, 15):

        @pl.when(slab + d < SLABS)
        def _(d=d):
            t_copy(d).start()

    send_c(1)
    after_b(2)
    send_c(2)
    l_wq.wait()
    project(0, 0, HALF, wq, q_v, False, 3)
    project(1, 0, HALF, wq, q_v, False, 3)

    first_head = mine_own // HD
    second_head = jnp.minimum(first_head + 1, 2)
    spot = lax.broadcasted_iota(jnp.int32, (PIECE, HD), 0) + mine_own
    in_first = spot < (first_head + 1) * HD

    def blank(n):
        weight[n] = jnp.zeros((PIECE, HD), F32)
        tbuf[n] = jnp.zeros((PIECE, HD), BF16)

    repeat(slab, SLABS, blank)

    def weigh(n, total):
        before = slab - 1 - n
        weight[before] = total
        wait_for(tdec.at[before], dec_recv.at[before])
        a = tdec[before, pl.ds(core * 3 + first_head, 1), :]
        b = tdec[before, pl.ds(core * 3 + second_head, 1), :]
        return jnp.where(in_first, a, b) * total

    lax.fori_loop(0, slab, weigh, jnp.ones((PIECE, HD), F32))
    after_c(0)
    repeat(0, slab, lambda n: wait_for(tbuf.at[n], t_recv.at[n]))
    total = weight[0] * tbuf[0].astype(F32)
    for n in range(1, SLABS - 1):
        total = total + weight[n] * tbuf[n].astype(F32)
    inc[pl.ds(mine, PIECE), :] = total.astype(BF16)

    def i_copy(d):
        held = inc.at[pl.ds(mine, PIECE)]
        return to_lon(held, held, i_send.at[d], i_recv, (lon + 2 * d) % LONS)

    repeat(1, LONS // 2, lambda d: i_copy(d).start())
    after_c(1)
    after_c(2)
    wait_for(inc.at[pl.ds(0, OWN - PIECE)], i_recv)
    held = inc.at[pl.ds(half, OWN)]
    e_copy = to_lon(held, held, e_send, e_recv, partner)
    e_copy.start()
    for p in range(3):
        d_copy(p).wait_recv()
    e_copy.wait_recv()

    l_gain.wait()

    def read(f):
        rows = pl.ds(f * 2 * LAT, 2 * LAT)
        alive = jnp.where(f < n_live, 1.0, 0.0).astype(F32)
        heads = []
        for h in range(HEADS):
            at = pl.ds(h * HD, HD)
            state = states[f, at, :].astype(F32) + reach[pl.ds(f * HEADS + h, 1), :] * inc[
                at, :
            ].astype(F32)
            readout = dot(q_v[:, rows, at].reshape(TOK, HD), state.astype(BF16))
            inverse = lax.rsqrt(jnp.mean(readout * readout, axis=-1, keepdims=True) + 1e-05)
            scale = gain[pl.ds(h * HD, HD)].reshape(1, HD) * alive
            heads.append((readout * inverse * scale).astype(BF16))
        back = dot(order[...], jnp.concatenate(heads, axis=1))
        normed[f * TOK : (f + 1) * TOK, :] = back.astype(BF16)

    for f in range(FRAMES):
        read(f)

    l_wo.wait()
    out_rows = out_v.reshape(FRAMES * TOK, D)

    def out_copy(j):
        lanes = pl.ds(pl.multiple_of(j * CHUNK, CHUNK), CHUNK)
        return pltpu.make_async_copy(
            out_v.at[:, :, :, lanes], out_hbm.at[:, :, :, lanes], out_sem.at[j]
        )

    def emit(j):
        lanes = pl.ds(pl.multiple_of(j * CHUNK, CHUNK), CHUNK)
        out_rows[:, lanes] = dot(normed[...], wo[:, lanes]).astype(BF16)
        out_copy(j).start()

    repeat(0, D // CHUNK, emit, 2)

    for f in range(FRAMES):
        for side in range(2):
            halo_copy(side, f).wait_send()
    for p in range(3):
        a_copy(p).wait_send()
        repeat(1, CHIPS, lambda d, p=p: b_copy(p, d).wait_send())
        repeat(1, CHIPS, lambda d, p=p: c_copy(p, d).wait_send())
        d_copy(p).wait_send()
    repeat(1, SLABS - slab, lambda d: dec_copy(d).wait_send())
    repeat(1, SLABS - slab, lambda d: t_copy(d).wait_send())
    repeat(1, LONS // 2, lambda d: i_copy(d).wait_send())
    e_copy.wait_send()
    repeat(0, D // CHUNK, lambda j: out_copy(j).wait())


def out_kernel(in_hbm, out_hbm, held, in_sem, out_sem):
    fetches = [pltpu.make_async_copy(in_hbm.at[f], held.at[f], in_sem.at[f]) for f in range(FRAMES)]
    stores = [pltpu.make_async_copy(held.at[f], out_hbm.at[f], out_sem.at[f]) for f in range(FRAMES)]
    for copy in fetches:
        copy.start()
    for fetch, store in zip(fetches, stores):
        fetch.wait()
        store.start()
    for copy in stores:
        copy.wait()


def local(frames_in, conv_kernel, w_query, w_key, w_value, w_out, norm_gain, log_gate, cam_valid, live_frames):
    dma = pltpu.SemaphoreType.DMA
    anywhere = pl.BlockSpec(memory_space=pltpu.HBM)
    held = pl.BlockSpec(memory_space=pltpu.VMEM)
    result = pl.pallas_call(
        kernel,
        out_shape=jax.ShapeDtypeStruct((FRAMES, LAT, COLS, D), BF16),
        in_specs=[anywhere] * 10,
        out_specs=anywhere,
        scratch_shapes=[
            pltpu.SMEM((1,), jnp.int32),
            pltpu.VMEM((FRAMES, LAT, COLS, D), BF16),
            pltpu.VMEM((3, 3, D), F32),
            pltpu.VMEM((D, HK), BF16),
            pltpu.VMEM((D, HK), BF16),
            pltpu.VMEM((D, HK), BF16),
            pltpu.VMEM((HK, D), BF16),
            pltpu.VMEM((HK,), F32),
            pltpu.VMEM((FRAMES, HEADS), F32),
            pltpu.VMEM((FRAMES, CAMS), jnp.int32),
            pltpu.VMEM((3 * TOK, TOK), BF16),
            pltpu.VMEM((3 * LAT, LAT), BF16),
            pltpu.VMEM((TOK, TOK), BF16),
            pltpu.VMEM((2, FRAMES, LAT, D), BF16),
            pltpu.VMEM((2, FRAMES, LAT, D), BF16),
            pltpu.VMEM((HALF, D), F32),
            pltpu.VMEM((2, HALF, D), BF16),
            pltpu.VMEM((2, HALF, HK), BF16),
            pltpu.VMEM((2, HALF, HK), BF16),
            pltpu.VMEM((2, HALF, HK), BF16),
            pltpu.VMEM((2, HALF, HD), F32),
            pltpu.VMEM((FRAMES * HEADS, HD), F32),
            pltpu.VMEM((FRAMES * HEADS, HD), F32),
            pltpu.VMEM((FRAMES, OWN, HD), BF16),
            pltpu.VMEM((OWN, HD), F32),
            pltpu.VMEM((FRAMES, OWN, HD), F32),
            pltpu.VMEM((OWN, HD), F32),
            pltpu.VMEM((FRAMES, OWN, HD), BF16),
            pltpu.VMEM((FRAMES, OWN, HD), BF16),
            pltpu.VMEM((CHIPS - 1, FRAMES, PIECE, HD), BF16),
            pltpu.VMEM((SLABS, PIECE, HD), BF16),
            pltpu.VMEM((8, HD), F32),
            pltpu.VMEM((SLABS, 8, HD), F32),
            pltpu.VMEM((SLABS, PIECE, HD), F32),
            pltpu.VMEM((FRAMES, HK, HD), BF16),
            pltpu.VMEM((HK, HD), BF16),
            pltpu.VMEM((FRAMES * TOK, HK), BF16),
            pltpu.VMEM((FRAMES, LAT, COLS, D), BF16),
            dma((13,)),
            dma((D // CHUNK,)),

            dma((2, FRAMES)),
            dma((2, FRAMES)),
            dma((3,)),
            dma((3,)),
            dma((3, CHIPS)),
            dma((3,)),
            dma((SLABS,)),
            dma((SLABS,)),
            dma((SLABS,)),
            dma((SLABS,)),
            dma((3, CHIPS)),
            dma((3,)),
            dma((3,)),
            dma((3,)),
            dma((LONS // 2,)),
            dma,
            dma,
            dma,
        ],
        compiler_params=pltpu.CompilerParams(
            collective_id=0, has_side_effects=True, vmem_limit_bytes=59392 * 1024
        ),
    )(frames_in, conv_kernel, w_query, w_key, w_value, w_out, norm_gain, log_gate, cam_valid, live_frames)
    return pl.pallas_call(
        out_kernel,
        out_shape=jax.ShapeDtypeStruct((FRAMES, LAT, COLS, D), BF16),
        in_specs=[anywhere],
        out_specs=anywhere,
        scratch_shapes=[
            pltpu.VMEM((FRAMES, LAT, COLS, D), BF16),
            dma((FRAMES,)),
            dma((FRAMES,)),
        ],
        compiler_params=pltpu.CompilerParams(vmem_limit_bytes=60 * 1024 * 1024),
    )(result)


def solution(mesh):
    in_specs = (
        P("tm", None, "lon", None),
        P(),
        P(),
        P(),
        P(),
        P(),
        P(),
        P("tm", None),
        P("tm", None),
        P("tm"),
    )
    out_specs = P("tm", None, "lon", None)
    return jax.shard_map(local, mesh=mesh, in_specs=in_specs, out_specs=out_specs, check_vma=False)
```

```python
import jax
import jax.numpy as jnp
from jax import lax
from jax.experimental import pallas as pl
from jax.experimental.pallas import tpu as pltpu
from jax.sharding import PartitionSpec as P

MESH = pl.DeviceIdType.MESH
F32 = jnp.float32
BF16 = jnp.bfloat16

HEADS = 6
HD = 128
CAMS = 6
FRAMES = 4
LAT = 32
COLS = 4
D = 1536
HK = HEADS * HD
TOK = LAT * COLS
LONG = 64
CHUNK = 256
HALF = FRAMES * 2 * LAT
OWN = HK // 2
CHIPS = 8
PIECE = OWN // CHIPS
PARTS = ((0, 1), (3,), (2,))
EARLY = 2
GATHERS = ((0, EARLY), (EARLY, FRAMES - EARLY + 1))
SLABS = 16
LONS = 16


def repeat(first, last, body, unroll=1):
    def step(i, carry):
        body(i)
        return carry

    lax.fori_loop(first, last, step, 0, unroll=unroll)


def dot(a, b):
    return jnp.dot(a, b, preferred_element_type=F32)


def column_of(t):
    block = t // LAT
    return jnp.where(block == 0, 1, jnp.where(block == 1, 2, jnp.where(block == 2, 0, 3)))


def kernel(
    x_hbm,
    ck_hbm,
    wq_hbm,
    wk_hbm,
    wv_hbm,
    wo_hbm,
    gain_hbm,
    lg_hbm,
    cam_hbm,
    live_hbm,
    out_hbm,
    live_ref,
    x_v,
    ck,
    wq,
    wk,
    wv,
    wo,
    gain,
    lg,
    cam,
    shift3,
    shift_h,
    order,
    edge_out,
    edge_in,
    partial,
    mixed,
    q_v,
    k_v,
    v_v,
    keep,
    dec,
    reach,
    other,
    other_sum,
    own,
    own_sum,
    abuf,
    bsend,
    bbuf,
    tsend,
    tbuf,
    dsend,
    tdec,
    weight,
    states,
    normed,
    out_v,
    load_sem,
    out_sem,

    halo_send,
    halo_recv,
    a_send,
    a_recv,
    b_send,
    b_recv,
    dec_send,
    dec_recv,
    t_send,
    t_recv,
    c_send,
    c_recv,
    d_send,
    d_recv,
):
    lon = lax.axis_index("lon")
    slab = lax.axis_index("tm")
    core = lon % 2
    chip = lon // 2
    partner = lon + 1 - 2 * core
    half = pl.multiple_of(core * OWN, OWN)
    mine_own = pl.multiple_of(chip * PIECE, 16)
    mine = pl.multiple_of(core * OWN + chip * PIECE, 16)

    loads = []
    for n, (src, dst) in enumerate(
        (
            (x_hbm.at[0], x_v.at[0]),
            (live_hbm, live_ref),
            (lg_hbm, lg),
            (cam_hbm, cam),
            (x_hbm.at[1], x_v.at[1]),
            (x_hbm.at[2], x_v.at[2]),
            (x_hbm.at[3], x_v.at[3]),
            (ck_hbm, ck),
            (gain_hbm, gain),
            (wk_hbm, wk),
            (wv_hbm, wv),
            (wq_hbm, wq),
            (wo_hbm, wo),
        )
    ):
        copy = pltpu.make_async_copy(src, dst, load_sem.at[n])
        copy.start()
        loads.append(copy)
    l_x0, l_live, l_lg, l_cam, l_x1, l_x2, l_x3, l_ck, l_gain, l_wk, l_wv, l_wq, l_wo = loads
    l_x = (l_x0, l_x1, l_x2, l_x3)

    barrier = pltpu.get_barrier_semaphore()

    def greet(d):
        pl.semaphore_signal(
            barrier, inc=1, device_id={"lon": (lon + d) % LONS}, device_id_type=MESH
        )
        pl.semaphore_signal(
            barrier, inc=1, device_id={"tm": (slab + d) % SLABS}, device_id_type=MESH
        )

    repeat(1, LONS, greet)

    def to_lon(src, dst, send, recv, target):
        return pltpu.make_async_remote_copy(
            src_ref=src,
            dst_ref=dst,
            send_sem=send,
            recv_sem=recv,
            device_id={"lon": target},
            device_id_type=MESH,
        )

    def wait_for(held, sem):
        pltpu.make_async_copy(held, held, sem).wait()

    row = lax.broadcasted_iota(jnp.int32, (TOK, TOK), 0)
    col = lax.broadcasted_iota(jnp.int32, (TOK, TOK), 1)
    c_row = column_of(row)
    for i in range(3):
        lat = row % LAT + (i - 1)
        hit = (lat >= 0) & (lat < LAT) & (col == lat * COLS + c_row)
        shift3[i * TOK : (i + 1) * TOK, :] = jnp.where(hit, 1.0, 0.0).astype(BF16)
    hit = row == (col % LAT) * COLS + column_of(col)
    order[...] = jnp.where(hit, 1.0, 0.0).astype(BF16)
    row = lax.broadcasted_iota(jnp.int32, (3 * LAT, LAT), 0)
    col = lax.broadcasted_iota(jnp.int32, (3 * LAT, LAT), 1)
    shift_h[...] = jnp.where(col == row % LAT + row // LAT - 1, 1.0, 0.0).astype(BF16)

    l_live.wait()
    l_lg.wait()
    l_cam.wait()
    n_live = live_ref[0]
    frame = lax.broadcasted_iota(jnp.int32, (FRAMES, HEADS), 0)
    live = jnp.where(frame < n_live, 1.0, 0.0).astype(F32)
    decay = jnp.exp(lg[...] * live)
    sofar = decay[0:1]
    for f in range(FRAMES):
        if f:
            sofar = sofar * decay[f : f + 1]
        for h in range(HEADS):
            at = f * HEADS + h
            dec[at : at + 1, :] = jnp.broadcast_to(decay[f : f + 1, h : h + 1], (1, HD))
            reach[at : at + 1, :] = jnp.broadcast_to(sofar[:, h : h + 1], (1, HD))
    dsend[...] = jnp.concatenate(
        [reach[(FRAMES - 1) * HEADS :, :], jnp.zeros((8 - HEADS, HD), F32)], axis=0
    )

    valid = cam[...].astype(F32) * live
    lane = lax.broadcasted_iota(jnp.int32, (1, CAMS), 1)
    for n, c in enumerate((1, 2, 0, 3)):
        camera = ((lon * COLS + c) * CAMS) // LONG
        for f in range(FRAMES):
            bit = jnp.sum(jnp.where(lane == camera, valid[f : f + 1], 0.0), axis=1, keepdims=True)
            at = f * 2 * LAT + (n % 2) * LAT
            keep[n // 2, at : at + LAT, :] = jnp.broadcast_to(bit, (LAT, HD))

    def dec_copy(d):
        return pltpu.make_async_remote_copy(
            src_ref=dsend,
            dst_ref=tdec.at[slab],
            send_sem=dec_send.at[d],
            recv_sem=dec_recv.at[slab],
            device_id={"tm": slab + d},
            device_id_type=MESH,
        )

    x_rows = x_v.reshape(FRAMES * TOK, D)

    def halo_copy(side, f):
        target = (lon + (1 if side == 0 else LONS - 1)) % LONS
        return to_lon(
            edge_out.at[side, f],
            edge_in.at[side, f],
            halo_send.at[side, f],
            halo_recv.at[side, f],
            target,
        )

    for f in range(FRAMES):
        l_x[f].wait()

        def extract(j, f=f):
            lanes = pl.ds(pl.multiple_of(j * CHUNK, CHUNK), CHUNK)
            planes = dot(shift3[TOK + 2 * LAT : 2 * TOK, :], x_rows[f * TOK : (f + 1) * TOK, lanes])
            planes = planes.astype(BF16)
            edge_out[1, f, :, lanes] = planes[:LAT]
            edge_out[0, f, :, lanes] = planes[LAT:]

        repeat(0, D // CHUNK, extract, 6)
        if f == 0:
            pl.semaphore_wait(barrier, 2 * (LONS - 1))
        for side in range(2):
            halo_copy(side, f).start()
    repeat(1, SLABS - slab, lambda d: dec_copy(d).start())

    l_ck.wait()

    def taps(j):
        lanes = pl.ds(pl.multiple_of(j * CHUNK, CHUNK), CHUNK)
        k = [[0.5 * ck[i, n : n + 1, lanes] for n in range(3)] for i in range(3)]

        def one(f):
            x = x_rows[pl.ds(pl.multiple_of(f * TOK, TOK), TOK), lanes]
            s = [dot(shift3[i * TOK : (i + 1) * TOK, :], x) for i in range(3)]
            place = {1: 0, 2: 1, 0: 2, 3: 3}

            def plane(i, c):
                at = place[c] * LAT
                return s[i][at : at + LAT]

            at = pl.multiple_of(f * 2 * LAT, 2 * LAT)
            for n, c in enumerate((1, 2, 0, 3)):
                total = None
                for i in range(3):
                    for m in range(3):
                        if 0 <= c + m - 1 < COLS:
                            term = k[i][m] * plane(i, c + m - 1)
                            total = term if total is None else total + term
                rows = pl.ds(at + (n % 2) * LAT, LAT)
                if n < 2:
                    mixed[0, rows, lanes] = (total * jnp.tanh(total) + total).astype(BF16)
                else:
                    partial[rows, lanes] = total

        repeat(0, FRAMES, one, FRAMES)

    repeat(0, D // CHUNK, taps, 2)

    def project(side, first, count, weights, dst, masked, unroll):
        rows = pl.ds(first, count)

        def one(j):
            lanes = pl.ds(pl.multiple_of(j * CHUNK, CHUNK), CHUNK)
            r = dot(mixed[side, rows, :], weights[:, lanes])
            if masked:
                m = keep[side, rows, :]
                r = r * jnp.concatenate([m, m], axis=1)
            dst[side, rows, lanes] = r.astype(BF16)

        repeat(0, HK // CHUNK, one, unroll)

    l_wk.wait()
    project(0, 0, HALF, wk, k_v, True, 3)
    l_wv.wait()
    project(0, 0, HALF, wv, v_v, False, 3)

    def edge_taps(f):
        def one(j):
            lanes = pl.ds(pl.multiple_of(j * CHUNK, CHUNK), CHUNK)
            for side in range(2):
                s = dot(shift_h[...], edge_in[side, f, :, lanes])
                rows = pl.ds(f * 2 * LAT + side * LAT, LAT)
                total = partial[rows, lanes]
                for i in range(3):
                    tap = 0.5 * ck[i, 2 * side : 2 * side + 1, lanes]
                    total = total + tap * s[i * LAT : (i + 1) * LAT]
                mixed[1, rows, lanes] = (total * jnp.tanh(total) + total).astype(BF16)

        repeat(0, D // CHUNK, one, D // CHUNK)

    def scan_heads(frames, first, carried, put):
        def one(n):
            h = first + n
            lanes = pl.ds(pl.multiple_of(h * HD, HD), HD)
            at = pl.ds(pl.multiple_of(n * HD, HD), HD)
            total = None
            for f in frames:
                rows = pl.ds(f * 2 * LAT, 2 * LAT)
                keys = k_v[:, rows, lanes].reshape(TOK, HD)
                values = v_v[:, rows, lanes].reshape(TOK, HD)
                term = lax.dot_general(
                    keys, values, (((0,), (0,)), ((), ())), preferred_element_type=F32
                )
                if f:
                    before = carried[at, :] if total is None else total
                    term = term + dec[pl.ds(f * HEADS + h, 1), :] * before
                total = term
                put(f, at, total)
            carried[at, :] = total

        repeat(0, 3, one, 3)

    def put_other(f, at, total):
        other[f, at, :] = total.astype(BF16)

    def put_own(f, at, total):
        own[f, at, :] = total

    def frames_of(p):
        return pl.ds(PARTS[p][0], len(PARTS[p]))

    def a_copy(p):
        at = frames_of(p)
        return to_lon(other.at[at], abuf.at[at], a_send.at[p], a_recv.at[p], partner)

    def b_copy(p, d):
        to = (chip + d) % CHIPS
        rows = pl.ds(pl.multiple_of(to * PIECE, 16), PIECE)
        return to_lon(
            bsend.at[frames_of(p), rows],
            bbuf.at[d - 1, frames_of(p)],
            b_send.at[p, d],
            b_recv.at[p],
            2 * to + core,
        )

    def c_copy(p, d):
        held = states.at[pl.ds(*GATHERS[p]), pl.ds(mine, PIECE)]
        to = (chip + d) % CHIPS
        return to_lon(held, held, c_send.at[p, d], c_recv.at[p], 2 * to + core)

    def d_copy(p):
        held = states.at[pl.ds(*GATHERS[p]), pl.ds(half, OWN)]
        return to_lon(held, held, d_send.at[p], d_recv.at[p], partner)

    def t_copy(d):
        return pltpu.make_async_remote_copy(
            src_ref=tsend,
            dst_ref=tbuf.at[slab],
            send_sem=t_send.at[d],
            recv_sem=t_recv.at[slab],
            device_id={"tm": slab + d},
            device_id_type=MESH,
        )

    def after_a(p):
        a_copy(p).wait_recv()
        for f in PARTS[p]:
            for n in range(3):
                rows = pl.ds(n * HD, HD)
                total = own[f, rows, :] + abuf[f, rows, :].astype(F32)
                own[f, rows, :] = total
                bsend[f, rows, :] = total.astype(BF16)
        repeat(1, CHIPS, lambda d: b_copy(p, d).start())

    def after_b(p):
        wait_for(bbuf.at[:, frames_of(p)], b_recv.at[p])
        for f in PARTS[p]:
            total = own[f, pl.ds(mine_own, PIECE), :]
            for d in range(CHIPS - 1):
                total = total + bbuf[d, f].astype(F32)
            if f < EARLY:
                states[f, pl.ds(mine, PIECE), :] = total.astype(BF16)
            else:
                own[f, pl.ds(mine_own, PIECE), :] = total
            if f == FRAMES - 1:
                tsend[...] = total.astype(BF16)

    def send_c(p):
        repeat(1, CHIPS, lambda d: c_copy(p, d).start())

    def after_c(p):
        wait_for(states.at[pl.ds(*GATHERS[p]), pl.ds(0, OWN - PIECE)], c_recv.at[p])
        d_copy(p).start()

    for group in ((0, 1), (2, 3)):
        for f in group:
            for side in range(2):
                halo_copy(side, f).wait_recv()
            edge_taps(f)
        first = group[0] * 2 * LAT
        if first:
            after_a(0)
        project(1, first, 4 * LAT, wk, k_v, True, 3)
        project(1, first, 4 * LAT, wv, v_v, False, 3)
        scan_heads(group, (1 - core) * 3, other_sum, put_other)
        if first:
            a_copy(1).start()
            a_copy(2).start()
        else:
            a_copy(0).start()
        scan_heads(group, core * 3, own_sum, put_own)
    after_a(1)
    after_a(2)
    after_b(0)
    send_c(0)
    after_b(1)
    for d in (4, 12, 5, 3, 11, 13, 2, 6, 10, 14, 8, 1, 7, 9, 15):

        @pl.when(slab + d < SLABS)
        def _(d=d):
            t_copy(d).start()

    after_b(2)
    l_wq.wait()
    project(0, 0, HALF, wq, q_v, False, 3)
    project(1, 0, HALF, wq, q_v, False, 3)

    first_head = mine_own // HD
    second_head = jnp.minimum(first_head + 1, 2)
    spot = lax.broadcasted_iota(jnp.int32, (PIECE, HD), 0) + mine_own
    in_first = spot < (first_head + 1) * HD

    def blank(n):
        weight[n] = jnp.zeros((PIECE, HD), F32)
        tbuf[n] = jnp.zeros((PIECE, HD), BF16)

    repeat(slab, SLABS, blank)

    def weigh(n, total):
        before = slab - 1 - n
        weight[before] = total
        wait_for(tdec.at[before], dec_recv.at[before])
        a = tdec[before, pl.ds(core * 3 + first_head, 1), :]
        b = tdec[before, pl.ds(core * 3 + second_head, 1), :]
        return jnp.where(in_first, a, b) * total

    lax.fori_loop(0, slab, weigh, jnp.ones((PIECE, HD), F32))
    after_c(0)
    repeat(0, slab, lambda n: wait_for(tbuf.at[n], t_recv.at[n]))
    total = weight[0] * tbuf[0].astype(F32)
    for n in range(1, SLABS - 1):
        total = total + weight[n] * tbuf[n].astype(F32)
    states[FRAMES, pl.ds(mine, PIECE), :] = total.astype(BF16)
    for f in range(EARLY, FRAMES):
        a = reach[pl.ds(f * HEADS + core * 3 + first_head, 1), :]
        b = reach[pl.ds(f * HEADS + core * 3 + second_head, 1), :]
        state = own[f, pl.ds(mine_own, PIECE), :] + jnp.where(in_first, a, b) * total
        states[f, pl.ds(mine, PIECE), :] = state.astype(BF16)

    send_c(1)
    after_c(1)
    for p in range(2):
        d_copy(p).wait_recv()

    l_gain.wait()

    def read(f):
        rows = pl.ds(f * 2 * LAT, 2 * LAT)
        alive = jnp.where(f < n_live, 1.0, 0.0).astype(F32)
        heads = []
        for h in range(HEADS):
            at = pl.ds(h * HD, HD)
            state = states[f, at, :]
            if f < EARLY:
                brought = reach[f * HEADS + h : f * HEADS + h + 1, :] * states[FRAMES, at, :].astype(F32)
                state = (state.astype(F32) + brought).astype(BF16)
            readout = dot(q_v[:, rows, at].reshape(TOK, HD), state)
            inverse = lax.rsqrt(jnp.mean(readout * readout, axis=-1, keepdims=True) + 1e-05)
            scale = gain[pl.ds(h * HD, HD)].reshape(1, HD) * alive
            heads.append((readout * inverse * scale).astype(BF16))
        back = dot(order[...], jnp.concatenate(heads, axis=1))
        normed[f * TOK : (f + 1) * TOK, :] = back.astype(BF16)

    for f in range(FRAMES):
        read(f)

    l_wo.wait()
    out_rows = out_v.reshape(FRAMES * TOK, D)

    def out_copy(j):
        lanes = pl.ds(pl.multiple_of(j * CHUNK, CHUNK), CHUNK)
        return pltpu.make_async_copy(
            out_v.at[:, :, :, lanes], out_hbm.at[:, :, :, lanes], out_sem.at[j]
        )

    def emit(j):
        lanes = pl.ds(pl.multiple_of(j * CHUNK, CHUNK), CHUNK)
        out_rows[:, lanes] = dot(normed[...], wo[:, lanes]).astype(BF16)
        out_copy(j).start()

    repeat(0, D // CHUNK, emit, 2)

    for f in range(FRAMES):
        for side in range(2):
            halo_copy(side, f).wait_send()
    for p in range(3):
        a_copy(p).wait_send()
        repeat(1, CHIPS, lambda d, p=p: b_copy(p, d).wait_send())
    for p in range(2):
        repeat(1, CHIPS, lambda d, p=p: c_copy(p, d).wait_send())
        d_copy(p).wait_send()
    repeat(1, SLABS - slab, lambda d: dec_copy(d).wait_send())
    repeat(1, SLABS - slab, lambda d: t_copy(d).wait_send())
    repeat(0, D // CHUNK, lambda j: out_copy(j).wait())


def out_kernel(in_hbm, out_hbm, held, in_sem, out_sem):
    fetches = [pltpu.make_async_copy(in_hbm.at[f], held.at[f], in_sem.at[f]) for f in range(FRAMES)]
    stores = [pltpu.make_async_copy(held.at[f], out_hbm.at[f], out_sem.at[f]) for f in range(FRAMES)]
    for copy in fetches:
        copy.start()
    for fetch, store in zip(fetches, stores):
        fetch.wait()
        store.start()
    for copy in stores:
        copy.wait()


def local(frames_in, conv_kernel, w_query, w_key, w_value, w_out, norm_gain, log_gate, cam_valid, live_frames):
    dma = pltpu.SemaphoreType.DMA
    anywhere = pl.BlockSpec(memory_space=pltpu.HBM)
    held = pl.BlockSpec(memory_space=pltpu.VMEM)
    result = pl.pallas_call(
        kernel,
        out_shape=jax.ShapeDtypeStruct((FRAMES, LAT, COLS, D), BF16),
        in_specs=[anywhere] * 10,
        out_specs=anywhere,
        scratch_shapes=[
            pltpu.SMEM((1,), jnp.int32),
            pltpu.VMEM((FRAMES, LAT, COLS, D), BF16),
            pltpu.VMEM((3, 3, D), F32),
            pltpu.VMEM((D, HK), BF16),
            pltpu.VMEM((D, HK), BF16),
            pltpu.VMEM((D, HK), BF16),
            pltpu.VMEM((HK, D), BF16),
            pltpu.VMEM((HK,), F32),
            pltpu.VMEM((FRAMES, HEADS), F32),
            pltpu.VMEM((FRAMES, CAMS), jnp.int32),
            pltpu.VMEM((3 * TOK, TOK), BF16),
            pltpu.VMEM((3 * LAT, LAT), BF16),
            pltpu.VMEM((TOK, TOK), BF16),
            pltpu.VMEM((2, FRAMES, LAT, D), BF16),
            pltpu.VMEM((2, FRAMES, LAT, D), BF16),
            pltpu.VMEM((HALF, D), F32),
            pltpu.VMEM((2, HALF, D), BF16),
            pltpu.VMEM((2, HALF, HK), BF16),
            pltpu.VMEM((2, HALF, HK), BF16),
            pltpu.VMEM((2, HALF, HK), BF16),
            pltpu.VMEM((2, HALF, HD), F32),
            pltpu.VMEM((FRAMES * HEADS, HD), F32),
            pltpu.VMEM((FRAMES * HEADS, HD), F32),
            pltpu.VMEM((FRAMES, OWN, HD), BF16),
            pltpu.VMEM((OWN, HD), F32),
            pltpu.VMEM((FRAMES, OWN, HD), F32),
            pltpu.VMEM((OWN, HD), F32),
            pltpu.VMEM((FRAMES, OWN, HD), BF16),
            pltpu.VMEM((FRAMES, OWN, HD), BF16),
            pltpu.VMEM((CHIPS - 1, FRAMES, PIECE, HD), BF16),
            pltpu.VMEM((PIECE, HD), BF16),
            pltpu.VMEM((SLABS, PIECE, HD), BF16),
            pltpu.VMEM((8, HD), F32),
            pltpu.VMEM((SLABS, 8, HD), F32),
            pltpu.VMEM((SLABS, PIECE, HD), F32),
            pltpu.VMEM((FRAMES + 1, HK, HD), BF16),
            pltpu.VMEM((FRAMES * TOK, HK), BF16),
            pltpu.VMEM((FRAMES, LAT, COLS, D), BF16),
            dma((13,)),
            dma((D // CHUNK,)),

            dma((2, FRAMES)),
            dma((2, FRAMES)),
            dma((3,)),
            dma((3,)),
            dma((3, CHIPS)),
            dma((3,)),
            dma((SLABS,)),
            dma((SLABS,)),
            dma((SLABS,)),
            dma((SLABS,)),
            dma((3, CHIPS)),
            dma((3,)),
            dma((3,)),
            dma((3,)),
        ],
        compiler_params=pltpu.CompilerParams(
            collective_id=0, has_side_effects=True, vmem_limit_bytes=59392 * 1024
        ),
    )(frames_in, conv_kernel, w_query, w_key, w_value, w_out, norm_gain, log_gate, cam_valid, live_frames)
    return pl.pallas_call(
        out_kernel,
        out_shape=jax.ShapeDtypeStruct((FRAMES, LAT, COLS, D), BF16),
        in_specs=[anywhere],
        out_specs=anywhere,
        scratch_shapes=[
            pltpu.VMEM((FRAMES, LAT, COLS, D), BF16),
            dma((FRAMES,)),
            dma((FRAMES,)),
        ],
        compiler_params=pltpu.CompilerParams(vmem_limit_bytes=60 * 1024 * 1024),
    )(result)


def solution(mesh):
    in_specs = (
        P("tm", None, "lon", None),
        P(),
        P(),
        P(),
        P(),
        P(),
        P(),
        P("tm", None),
        P("tm", None),
        P("tm"),
    )
    out_specs = P("tm", None, "lon", None)
    return jax.shard_map(local, mesh=mesh, in_specs=in_specs, out_specs=out_specs, check_vma=False)
```

```python
import jax
import jax.numpy as jnp
from jax import lax
from jax.experimental import pallas as pl
from jax.experimental.pallas import tpu as pltpu
from jax.sharding import PartitionSpec as P

MESH = pl.DeviceIdType.MESH
F32 = jnp.float32
BF16 = jnp.bfloat16

HEADS = 6
HD = 128
CAMS = 6
FRAMES = 4
LAT = 32
COLS = 4
D = 1536
HK = HEADS * HD
TOK = LAT * COLS
LONG = 64
CHUNK = 256
HALF = FRAMES * 2 * LAT
OWN = HK // 2
CHIPS = 8
XS = 4
PIECE = OWN // CHIPS
PARTS = ((0, 1), (3,), (2,))
EARLY = 2
GATHERS = ((0, EARLY), (EARLY, FRAMES - EARLY + 1))
SLABS = 16
LONS = 16


def repeat(first, last, body, unroll=1):
    def step(i, carry):
        body(i)
        return carry

    lax.fori_loop(first, last, step, 0, unroll=unroll)


def dot(a, b):
    return jnp.dot(a, b, preferred_element_type=F32)


def column_of(t):
    block = t // LAT
    return jnp.where(block == 0, 1, jnp.where(block == 1, 2, jnp.where(block == 2, 0, 3)))


def kernel(
    x_hbm,
    ck_hbm,
    wq_hbm,
    wk_hbm,
    wv_hbm,
    wo_hbm,
    gain_hbm,
    lg_hbm,
    cam_hbm,
    live_hbm,
    out_hbm,
    live_ref,
    x_v,
    ck,
    wq,
    wk,
    wv,
    wo,
    gain,
    lg,
    cam,
    shift3,
    shift_h,
    order,
    edge_out,
    edge_in,
    partial,
    mixed,
    q_v,
    k_v,
    v_v,
    keep,
    dec,
    reach,
    other,
    other_sum,
    own,
    own_sum,
    abuf,
    bsend,
    bbuf,
    tsend,
    tbuf,
    dsend,
    tdec,
    weight,
    states,
    normed,
    out_v,
    load_sem,
    out_sem,

    halo_send,
    halo_recv,
    a_send,
    a_recv,
    b_send,
    b_recv,
    dec_send,
    dec_recv,
    t_send,
    t_recv,
    c_send,
    c_recv,
    across_recv,
    d_send,
    d_recv,
):
    lon = lax.axis_index("lon")
    slab = lax.axis_index("tm")
    core = lon % 2
    chip = lon // 2
    partner = lon + 1 - 2 * core
    half = pl.multiple_of(core * OWN, OWN)
    mine_own = pl.multiple_of(chip * PIECE, 16)
    mine = pl.multiple_of(core * OWN + chip * PIECE, 16)

    loads = []
    for n, (src, dst) in enumerate(
        (
            (x_hbm.at[0], x_v.at[0]),
            (live_hbm, live_ref),
            (lg_hbm, lg),
            (cam_hbm, cam),
            (x_hbm.at[1], x_v.at[1]),
            (x_hbm.at[2], x_v.at[2]),
            (x_hbm.at[3], x_v.at[3]),
            (ck_hbm, ck),
            (gain_hbm, gain),
            (wk_hbm, wk),
            (wv_hbm, wv),
            (wq_hbm, wq),
            (wo_hbm, wo),
        )
    ):
        copy = pltpu.make_async_copy(src, dst, load_sem.at[n])
        copy.start()
        loads.append(copy)
    l_x0, l_live, l_lg, l_cam, l_x1, l_x2, l_x3, l_ck, l_gain, l_wk, l_wv, l_wq, l_wo = loads
    l_x = (l_x0, l_x1, l_x2, l_x3)

    barrier = pltpu.get_barrier_semaphore()

    def greet(d):
        pl.semaphore_signal(
            barrier, inc=1, device_id={"lon": (lon + d) % LONS}, device_id_type=MESH
        )
        pl.semaphore_signal(
            barrier, inc=1, device_id={"tm": (slab + d) % SLABS}, device_id_type=MESH
        )

    repeat(1, LONS, greet)

    def to_lon(src, dst, send, recv, target):
        return pltpu.make_async_remote_copy(
            src_ref=src,
            dst_ref=dst,
            send_sem=send,
            recv_sem=recv,
            device_id={"lon": target},
            device_id_type=MESH,
        )

    def wait_for(held, sem):
        pltpu.make_async_copy(held, held, sem).wait()

    row = lax.broadcasted_iota(jnp.int32, (TOK, TOK), 0)
    col = lax.broadcasted_iota(jnp.int32, (TOK, TOK), 1)
    c_row = column_of(row)
    for i in range(3):
        lat = row % LAT + (i - 1)
        hit = (lat >= 0) & (lat < LAT) & (col == lat * COLS + c_row)
        shift3[i * TOK : (i + 1) * TOK, :] = jnp.where(hit, 1.0, 0.0).astype(BF16)
    hit = row == (col % LAT) * COLS + column_of(col)
    order[...] = jnp.where(hit, 1.0, 0.0).astype(BF16)
    row = lax.broadcasted_iota(jnp.int32, (3 * LAT, LAT), 0)
    col = lax.broadcasted_iota(jnp.int32, (3 * LAT, LAT), 1)
    shift_h[...] = jnp.where(col == row % LAT + row // LAT - 1, 1.0, 0.0).astype(BF16)

    l_live.wait()
    l_lg.wait()
    l_cam.wait()
    n_live = live_ref[0]
    frame = lax.broadcasted_iota(jnp.int32, (FRAMES, HEADS), 0)
    live = jnp.where(frame < n_live, 1.0, 0.0).astype(F32)
    decay = jnp.exp(lg[...] * live)
    sofar = decay[0:1]
    for f in range(FRAMES):
        if f:
            sofar = sofar * decay[f : f + 1]
        for h in range(HEADS):
            at = f * HEADS + h
            dec[at : at + 1, :] = jnp.broadcast_to(decay[f : f + 1, h : h + 1], (1, HD))
            reach[at : at + 1, :] = jnp.broadcast_to(sofar[:, h : h + 1], (1, HD))
    dsend[...] = jnp.concatenate(
        [reach[(FRAMES - 1) * HEADS :, :], jnp.zeros((8 - HEADS, HD), F32)], axis=0
    )

    valid = cam[...].astype(F32) * live
    lane = lax.broadcasted_iota(jnp.int32, (1, CAMS), 1)
    for n, c in enumerate((1, 2, 0, 3)):
        camera = ((lon * COLS + c) * CAMS) // LONG
        for f in range(FRAMES):
            bit = jnp.sum(jnp.where(lane == camera, valid[f : f + 1], 0.0), axis=1, keepdims=True)
            at = f * 2 * LAT + (n % 2) * LAT
            keep[n // 2, at : at + LAT, :] = jnp.broadcast_to(bit, (LAT, HD))

    def dec_copy(d):
        return pltpu.make_async_remote_copy(
            src_ref=dsend,
            dst_ref=tdec.at[slab],
            send_sem=dec_send.at[d],
            recv_sem=dec_recv.at[slab],
            device_id={"tm": slab + d},
            device_id_type=MESH,
        )

    x_rows = x_v.reshape(FRAMES * TOK, D)

    def halo_copy(side, f):
        target = (lon + (1 if side == 0 else LONS - 1)) % LONS
        return to_lon(
            edge_out.at[side, f],
            edge_in.at[side, f],
            halo_send.at[side, f],
            halo_recv.at[side, f],
            target,
        )

    for f in range(FRAMES):
        l_x[f].wait()

        def extract(j, f=f):
            lanes = pl.ds(pl.multiple_of(j * CHUNK, CHUNK), CHUNK)
            planes = dot(shift3[TOK + 2 * LAT : 2 * TOK, :], x_rows[f * TOK : (f + 1) * TOK, lanes])
            planes = planes.astype(BF16)
            edge_out[1, f, :, lanes] = planes[:LAT]
            edge_out[0, f, :, lanes] = planes[LAT:]

        repeat(0, D // CHUNK, extract, 6)
        if f == 0:
            pl.semaphore_wait(barrier, 2 * (LONS - 1))
        for side in range(2):
            halo_copy(side, f).start()
    repeat(1, SLABS - slab, lambda d: dec_copy(d).start())

    l_ck.wait()

    def taps(j):
        lanes = pl.ds(pl.multiple_of(j * CHUNK, CHUNK), CHUNK)
        k = [[0.5 * ck[i, n : n + 1, lanes] for n in range(3)] for i in range(3)]

        def one(f):
            x = x_rows[pl.ds(pl.multiple_of(f * TOK, TOK), TOK), lanes]
            s = [dot(shift3[i * TOK : (i + 1) * TOK, :], x) for i in range(3)]
            place = {1: 0, 2: 1, 0: 2, 3: 3}

            def plane(i, c):
                at = place[c] * LAT
                return s[i][at : at + LAT]

            at = pl.multiple_of(f * 2 * LAT, 2 * LAT)
            for n, c in enumerate((1, 2, 0, 3)):
                total = None
                for i in range(3):
                    for m in range(3):
                        if 0 <= c + m - 1 < COLS:
                            term = k[i][m] * plane(i, c + m - 1)
                            total = term if total is None else total + term
                rows = pl.ds(at + (n % 2) * LAT, LAT)
                if n < 2:
                    mixed[0, rows, lanes] = (total * jnp.tanh(total) + total).astype(BF16)
                else:
                    partial[rows, lanes] = total

        repeat(0, FRAMES, one, FRAMES)

    repeat(0, D // CHUNK, taps, 2)

    def project(side, first, count, weights, dst, masked, unroll):
        rows = pl.ds(first, count)

        def one(j):
            lanes = pl.ds(pl.multiple_of(j * CHUNK, CHUNK), CHUNK)
            r = dot(mixed[side, rows, :], weights[:, lanes])
            if masked:
                m = keep[side, rows, :]
                r = r * jnp.concatenate([m, m], axis=1)
            dst[side, rows, lanes] = r.astype(BF16)

        repeat(0, HK // CHUNK, one, unroll)

    l_wk.wait()
    project(0, 0, HALF, wk, k_v, True, 3)
    l_wv.wait()
    project(0, 0, HALF, wv, v_v, False, 3)

    def edge_taps(f):
        def one(j):
            lanes = pl.ds(pl.multiple_of(j * CHUNK, CHUNK), CHUNK)
            for side in range(2):
                s = dot(shift_h[...], edge_in[side, f, :, lanes])
                rows = pl.ds(f * 2 * LAT + side * LAT, LAT)
                total = partial[rows, lanes]
                for i in range(3):
                    tap = 0.5 * ck[i, 2 * side : 2 * side + 1, lanes]
                    total = total + tap * s[i * LAT : (i + 1) * LAT]
                mixed[1, rows, lanes] = (total * jnp.tanh(total) + total).astype(BF16)

        repeat(0, D // CHUNK, one, D // CHUNK)

    def scan_heads(frames, first, carried, put):
        def one(n):
            h = first + n
            lanes = pl.ds(pl.multiple_of(h * HD, HD), HD)
            at = pl.ds(pl.multiple_of(n * HD, HD), HD)
            total = None
            for f in frames:
                rows = pl.ds(f * 2 * LAT, 2 * LAT)
                keys = k_v[:, rows, lanes].reshape(TOK, HD)
                values = v_v[:, rows, lanes].reshape(TOK, HD)
                term = lax.dot_general(
                    keys, values, (((0,), (0,)), ((), ())), preferred_element_type=F32
                )
                if f:
                    before = carried[at, :] if total is None else total
                    term = term + dec[pl.ds(f * HEADS + h, 1), :] * before
                total = term
                put(f, at, total)
            carried[at, :] = total

        repeat(0, 3, one, 3)

    def put_other(f, at, total):
        other[f, at, :] = total.astype(BF16)

    def put_own(f, at, total):
        own[f, at, :] = total

    def frames_of(p):
        return pl.ds(PARTS[p][0], len(PARTS[p]))

    def a_copy(p):
        at = frames_of(p)
        return to_lon(other.at[at], abuf.at[at], a_send.at[p], a_recv.at[p], partner)

    def b_copy(p, d):
        to = (chip + d) % CHIPS
        rows = pl.ds(pl.multiple_of(to * PIECE, 16), PIECE)
        return to_lon(
            bsend.at[frames_of(p), rows],
            bbuf.at[d - 1, frames_of(p)],
            b_send.at[p, d],
            b_recv.at[p],
            2 * to + core,
        )

    def c_copy(p, d):
        held = states.at[pl.ds(*GATHERS[p]), pl.ds(mine, PIECE)]
        to = (chip + d) % CHIPS
        return to_lon(held, held, c_send.at[p, d], c_recv.at[p], 2 * to + core)

    def d_copy(p):
        held = states.at[pl.ds(*GATHERS[p]), pl.ds(half, OWN)]
        return to_lon(held, held, d_send.at[p], d_recv.at[p], partner)

    def t_copy(d):
        return pltpu.make_async_remote_copy(
            src_ref=tsend,
            dst_ref=tbuf.at[slab],
            send_sem=t_send.at[d],
            recv_sem=t_recv.at[slab],
            device_id={"tm": slab + d},
            device_id_type=MESH,
        )

    def after_a(p):
        a_copy(p).wait_recv()
        for f in PARTS[p]:
            for n in range(3):
                rows = pl.ds(n * HD, HD)
                total = own[f, rows, :] + abuf[f, rows, :].astype(F32)
                own[f, rows, :] = total
                bsend[f, rows, :] = total.astype(BF16)
        repeat(1, CHIPS, lambda d: b_copy(p, d).start())

    def after_b(p):
        wait_for(bbuf.at[:, frames_of(p)], b_recv.at[p])
        for f in PARTS[p]:
            total = own[f, pl.ds(mine_own, PIECE), :]
            for d in range(CHIPS - 1):
                total = total + bbuf[d, f].astype(F32)
            if f < EARLY:
                states[f, pl.ds(mine, PIECE), :] = total.astype(BF16)
            else:
                own[f, pl.ds(mine_own, PIECE), :] = total
            if f == FRAMES - 1:
                tsend[...] = total.astype(BF16)

    def send_c(p):
        repeat(1, CHIPS, lambda d: c_copy(p, d).start())

    def row_copy(at, k, sem):
        held = states.at[pl.ds(*GATHERS[0]), pl.ds(at, PIECE)]
        to = (chip // XS) * XS + (chip + k) % XS
        return to_lon(held, held, c_send.at[0, sem], c_recv.at[0], 2 * to + core)

    def across_copy():
        held = states.at[pl.ds(*GATHERS[0]), pl.ds(mine, PIECE)]
        to = (chip + XS) % CHIPS
        return to_lon(held, held, c_send.at[0, XS], across_recv, 2 * to + core)

    def send_early():
        across_copy().start()
        for k in range(1, XS):
            row_copy(mine, k, k).start()

    def pass_early():
        across_copy().wait_recv()
        at = pl.multiple_of(core * OWN + (chip + XS) % CHIPS * PIECE, 16)
        for k in range(1, XS):
            row_copy(at, k, XS + k).start()

    def after_c(p):
        pieces = OWN - PIECE if p else OWN - 2 * PIECE
        wait_for(states.at[pl.ds(*GATHERS[p]), pl.ds(0, pieces)], c_recv.at[p])
        d_copy(p).start()

    for group in ((0, 1), (2, 3)):
        for f in group:
            for side in range(2):
                halo_copy(side, f).wait_recv()
            edge_taps(f)
        first = group[0] * 2 * LAT
        if first:
            after_a(0)
        project(1, first, 4 * LAT, wk, k_v, True, 3)
        project(1, first, 4 * LAT, wv, v_v, False, 3)
        scan_heads(group, (1 - core) * 3, other_sum, put_other)
        if first:
            a_copy(1).start()
            a_copy(2).start()
        else:
            a_copy(0).start()
        scan_heads(group, core * 3, own_sum, put_own)
    after_a(1)
    after_a(2)
    after_b(0)
    send_early()
    after_b(1)
    for d in (4, 12, 5, 3, 11, 13, 2, 6, 10, 14, 8, 1, 7, 9, 15):

        @pl.when(slab + d < SLABS)
        def _(d=d):
            t_copy(d).start()

    after_b(2)
    l_wq.wait()
    project(0, 0, HALF, wq, q_v, False, 3)
    project(1, 0, HALF, wq, q_v, False, 3)

    first_head = mine_own // HD
    second_head = jnp.minimum(first_head + 1, 2)
    spot = lax.broadcasted_iota(jnp.int32, (PIECE, HD), 0) + mine_own
    in_first = spot < (first_head + 1) * HD

    def blank(n):
        weight[n] = jnp.zeros((PIECE, HD), F32)
        tbuf[n] = jnp.zeros((PIECE, HD), BF16)

    repeat(slab, SLABS, blank)

    def weigh(n, total):
        before = slab - 1 - n
        weight[before] = total
        wait_for(tdec.at[before], dec_recv.at[before])
        a = tdec[before, pl.ds(core * 3 + first_head, 1), :]
        b = tdec[before, pl.ds(core * 3 + second_head, 1), :]
        return jnp.where(in_first, a, b) * total

    lax.fori_loop(0, slab, weigh, jnp.ones((PIECE, HD), F32))
    pass_early()
    repeat(0, slab, lambda n: wait_for(tbuf.at[n], t_recv.at[n]))
    total = weight[0] * tbuf[0].astype(F32)
    for n in range(1, SLABS - 1):
        total = total + weight[n] * tbuf[n].astype(F32)
    states[FRAMES, pl.ds(mine, PIECE), :] = total.astype(BF16)
    for f in range(EARLY, FRAMES):
        a = reach[pl.ds(f * HEADS + core * 3 + first_head, 1), :]
        b = reach[pl.ds(f * HEADS + core * 3 + second_head, 1), :]
        state = own[f, pl.ds(mine_own, PIECE), :] + jnp.where(in_first, a, b) * total
        states[f, pl.ds(mine, PIECE), :] = state.astype(BF16)

    send_c(1)
    after_c(0)
    after_c(1)
    for p in range(2):
        d_copy(p).wait_recv()

    l_gain.wait()

    def read(f):
        rows = pl.ds(f * 2 * LAT, 2 * LAT)
        alive = jnp.where(f < n_live, 1.0, 0.0).astype(F32)
        heads = []
        for h in range(HEADS):
            at = pl.ds(h * HD, HD)
            state = states[f, at, :]
            if f < EARLY:
                brought = reach[f * HEADS + h : f * HEADS + h + 1, :] * states[FRAMES, at, :].astype(F32)
                state = (state.astype(F32) + brought).astype(BF16)
            readout = dot(q_v[:, rows, at].reshape(TOK, HD), state)
            inverse = lax.rsqrt(jnp.mean(readout * readout, axis=-1, keepdims=True) + 1e-05)
            scale = gain[pl.ds(h * HD, HD)].reshape(1, HD) * alive
            heads.append((readout * inverse * scale).astype(BF16))
        back = dot(order[...], jnp.concatenate(heads, axis=1))
        normed[f * TOK : (f + 1) * TOK, :] = back.astype(BF16)

    for f in range(FRAMES):
        read(f)

    l_wo.wait()
    out_rows = out_v.reshape(FRAMES * TOK, D)

    def out_copy(j):
        lanes = pl.ds(pl.multiple_of(j * CHUNK, CHUNK), CHUNK)
        return pltpu.make_async_copy(
            out_v.at[:, :, :, lanes], out_hbm.at[:, :, :, lanes], out_sem.at[j]
        )

    def emit(j):
        lanes = pl.ds(pl.multiple_of(j * CHUNK, CHUNK), CHUNK)
        out_rows[:, lanes] = dot(normed[...], wo[:, lanes]).astype(BF16)
        out_copy(j).start()

    repeat(0, D // CHUNK, emit, 2)

    for f in range(FRAMES):
        for side in range(2):
            halo_copy(side, f).wait_send()
    for p in range(3):
        a_copy(p).wait_send()
        repeat(1, CHIPS, lambda d, p=p: b_copy(p, d).wait_send())
    for p in range(2):
        repeat(1, CHIPS, lambda d, p=p: c_copy(p, d).wait_send())
        d_copy(p).wait_send()
    repeat(1, SLABS - slab, lambda d: dec_copy(d).wait_send())
    repeat(1, SLABS - slab, lambda d: t_copy(d).wait_send())
    repeat(0, D // CHUNK, lambda j: out_copy(j).wait())


def out_kernel(in_hbm, out_hbm, held, in_sem, out_sem):
    fetches = [pltpu.make_async_copy(in_hbm.at[f], held.at[f], in_sem.at[f]) for f in range(FRAMES)]
    stores = [pltpu.make_async_copy(held.at[f], out_hbm.at[f], out_sem.at[f]) for f in range(FRAMES)]
    for copy in fetches:
        copy.start()
    for fetch, store in zip(fetches, stores):
        fetch.wait()
        store.start()
    for copy in stores:
        copy.wait()


def local(frames_in, conv_kernel, w_query, w_key, w_value, w_out, norm_gain, log_gate, cam_valid, live_frames):
    dma = pltpu.SemaphoreType.DMA
    anywhere = pl.BlockSpec(memory_space=pltpu.HBM)
    held = pl.BlockSpec(memory_space=pltpu.VMEM)
    result = pl.pallas_call(
        kernel,
        out_shape=jax.ShapeDtypeStruct((FRAMES, LAT, COLS, D), BF16),
        in_specs=[anywhere] * 10,
        out_specs=anywhere,
        scratch_shapes=[
            pltpu.SMEM((1,), jnp.int32),
            pltpu.VMEM((FRAMES, LAT, COLS, D), BF16),
            pltpu.VMEM((3, 3, D), F32),
            pltpu.VMEM((D, HK), BF16),
            pltpu.VMEM((D, HK), BF16),
            pltpu.VMEM((D, HK), BF16),
            pltpu.VMEM((HK, D), BF16),
            pltpu.VMEM((HK,), F32),
            pltpu.VMEM((FRAMES, HEADS), F32),
            pltpu.VMEM((FRAMES, CAMS), jnp.int32),
            pltpu.VMEM((3 * TOK, TOK), BF16),
            pltpu.VMEM((3 * LAT, LAT), BF16),
            pltpu.VMEM((TOK, TOK), BF16),
            pltpu.VMEM((2, FRAMES, LAT, D), BF16),
            pltpu.VMEM((2, FRAMES, LAT, D), BF16),
            pltpu.VMEM((HALF, D), F32),
            pltpu.VMEM((2, HALF, D), BF16),
            pltpu.VMEM((2, HALF, HK), BF16),
            pltpu.VMEM((2, HALF, HK), BF16),
            pltpu.VMEM((2, HALF, HK), BF16),
            pltpu.VMEM((2, HALF, HD), F32),
            pltpu.VMEM((FRAMES * HEADS, HD), F32),
            pltpu.VMEM((FRAMES * HEADS, HD), F32),
            pltpu.VMEM((FRAMES, OWN, HD), BF16),
            pltpu.VMEM((OWN, HD), F32),
            pltpu.VMEM((FRAMES, OWN, HD), F32),
            pltpu.VMEM((OWN, HD), F32),
            pltpu.VMEM((FRAMES, OWN, HD), BF16),
            pltpu.VMEM((FRAMES, OWN, HD), BF16),
            pltpu.VMEM((CHIPS - 1, FRAMES, PIECE, HD), BF16),
            pltpu.VMEM((PIECE, HD), BF16),
            pltpu.VMEM((SLABS, PIECE, HD), BF16),
            pltpu.VMEM((8, HD), F32),
            pltpu.VMEM((SLABS, 8, HD), F32),
            pltpu.VMEM((SLABS, PIECE, HD), F32),
            pltpu.VMEM((FRAMES + 1, HK, HD), BF16),
            pltpu.VMEM((FRAMES * TOK, HK), BF16),
            pltpu.VMEM((FRAMES, LAT, COLS, D), BF16),
            dma((13,)),
            dma((D // CHUNK,)),

            dma((2, FRAMES)),
            dma((2, FRAMES)),
            dma((3,)),
            dma((3,)),
            dma((3, CHIPS)),
            dma((3,)),
            dma((SLABS,)),
            dma((SLABS,)),
            dma((SLABS,)),
            dma((SLABS,)),
            dma((3, CHIPS)),
            dma((3,)),
            dma,
            dma((3,)),
            dma((3,)),
        ],
        compiler_params=pltpu.CompilerParams(
            collective_id=0, has_side_effects=True, vmem_limit_bytes=59392 * 1024
        ),
    )(frames_in, conv_kernel, w_query, w_key, w_value, w_out, norm_gain, log_gate, cam_valid, live_frames)
    return pl.pallas_call(
        out_kernel,
        out_shape=jax.ShapeDtypeStruct((FRAMES, LAT, COLS, D), BF16),
        in_specs=[anywhere],
        out_specs=anywhere,
        scratch_shapes=[
            pltpu.VMEM((FRAMES, LAT, COLS, D), BF16),
            dma((FRAMES,)),
            dma((FRAMES,)),
        ],
        compiler_params=pltpu.CompilerParams(vmem_limit_bytes=60 * 1024 * 1024),
    )(result)


def solution(mesh):
    in_specs = (
        P("tm", None, "lon", None),
        P(),
        P(),
        P(),
        P(),
        P(),
        P(),
        P("tm", None),
        P("tm", None),
        P("tm"),
    )
    out_specs = P("tm", None, "lon", None)
    return jax.shard_map(local, mesh=mesh, in_specs=in_specs, out_specs=out_specs, check_vma=False)
```

```python
import jax
import jax.numpy as jnp
from jax import lax
from jax.experimental import pallas as pl
from jax.experimental.pallas import tpu as pltpu
from jax.sharding import PartitionSpec as P

MESH = pl.DeviceIdType.MESH
F32 = jnp.float32
BF16 = jnp.bfloat16

HEADS = 6
HD = 128
CAMS = 6
FRAMES = 4
LAT = 32
COLS = 4
D = 1536
HK = HEADS * HD
TOK = LAT * COLS
LONG = 64
CHUNK = 256
HALF = FRAMES * 2 * LAT
OWN = HK // 2
CHIPS = 8
XS = 4
PIECE = OWN // CHIPS
PARTS = ((0, 1), (3,), (2,))
EARLY = 2
GATHERS = ((0, EARLY), (EARLY, FRAMES - EARLY + 1))
SLABS = 16
LONS = 16


def repeat(first, last, body, unroll=1):
    def step(i, carry):
        body(i)
        return carry

    lax.fori_loop(first, last, step, 0, unroll=unroll)


def dot(a, b):
    return jnp.dot(a, b, preferred_element_type=F32)


def column_of(t):
    block = t // LAT
    return jnp.where(block == 0, 1, jnp.where(block == 1, 2, jnp.where(block == 2, 0, 3)))


def kernel(
    x_hbm,
    ck_hbm,
    wq_hbm,
    wk_hbm,
    wv_hbm,
    wo_hbm,
    gain_hbm,
    lg_hbm,
    cam_hbm,
    live_hbm,
    out_hbm,
    live_ref,
    x_v,
    ck,
    wq,
    wk,
    wv,
    wo,
    gain,
    lg,
    cam,
    shift3,
    shift_h,
    order,
    edge_out,
    edge_in,
    partial,
    mixed,
    q_v,
    k_v,
    v_v,
    keep,
    dec,
    reach,
    other,
    other_sum,
    own,
    own_sum,
    abuf,
    bsend,
    bbuf,
    tsend,
    tbuf,
    dsend,
    tdec,
    weight,
    states,
    normed,
    out_v,
    load_sem,
    out_sem,

    halo_send,
    halo_recv,
    a_send,
    a_recv,
    b_send,
    b_recv,
    dec_send,
    dec_recv,
    t_send,
    t_recv,
    c_send,
    c_recv,
    across_recv,
    d_send,
    d_recv,
):
    lon = lax.axis_index("lon")
    slab = lax.axis_index("tm")
    core = lon % 2
    chip = lon // 2
    partner = lon + 1 - 2 * core
    half = pl.multiple_of(core * OWN, OWN)
    mine_own = pl.multiple_of(chip * PIECE, 16)
    mine = pl.multiple_of(core * OWN + chip * PIECE, 16)

    loads = []
    for n, (src, dst) in enumerate(
        (
            (x_hbm.at[0], x_v.at[0]),
            (live_hbm, live_ref),
            (lg_hbm, lg),
            (cam_hbm, cam),
            (x_hbm.at[1], x_v.at[1]),
            (x_hbm.at[2], x_v.at[2]),
            (x_hbm.at[3], x_v.at[3]),
            (ck_hbm, ck),
            (gain_hbm, gain),
            (wk_hbm, wk),
            (wv_hbm, wv),
            (wq_hbm, wq),
            (wo_hbm, wo),
        )
    ):
        copy = pltpu.make_async_copy(src, dst, load_sem.at[n])
        copy.start()
        loads.append(copy)
    l_x0, l_live, l_lg, l_cam, l_x1, l_x2, l_x3, l_ck, l_gain, l_wk, l_wv, l_wq, l_wo = loads
    l_x = (l_x0, l_x1, l_x2, l_x3)

    barrier = pltpu.get_barrier_semaphore()

    def greet(d):
        pl.semaphore_signal(
            barrier, inc=1, device_id={"lon": (lon + d) % LONS}, device_id_type=MESH
        )
        pl.semaphore_signal(
            barrier, inc=1, device_id={"tm": (slab + d) % SLABS}, device_id_type=MESH
        )

    repeat(1, LONS, greet)

    def to_lon(src, dst, send, recv, target):
        return pltpu.make_async_remote_copy(
            src_ref=src,
            dst_ref=dst,
            send_sem=send,
            recv_sem=recv,
            device_id={"lon": target},
            device_id_type=MESH,
        )

    def wait_for(held, sem):
        pltpu.make_async_copy(held, held, sem).wait()

    row = lax.broadcasted_iota(jnp.int32, (TOK, TOK), 0)
    col = lax.broadcasted_iota(jnp.int32, (TOK, TOK), 1)
    c_row = column_of(row)
    for i in range(3):
        lat = row % LAT + (i - 1)
        hit = (lat >= 0) & (lat < LAT) & (col == lat * COLS + c_row)
        shift3[i * TOK : (i + 1) * TOK, :] = jnp.where(hit, 1.0, 0.0).astype(BF16)
    hit = row == (col % LAT) * COLS + column_of(col)
    order[...] = jnp.where(hit, 1.0, 0.0).astype(BF16)
    row = lax.broadcasted_iota(jnp.int32, (3 * LAT, LAT), 0)
    col = lax.broadcasted_iota(jnp.int32, (3 * LAT, LAT), 1)
    shift_h[...] = jnp.where(col == row % LAT + row // LAT - 1, 1.0, 0.0).astype(BF16)

    l_live.wait()
    l_lg.wait()
    l_cam.wait()
    n_live = live_ref[0]
    frame = lax.broadcasted_iota(jnp.int32, (FRAMES, HEADS), 0)
    live = jnp.where(frame < n_live, 1.0, 0.0).astype(F32)
    decay = jnp.exp(lg[...] * live)
    sofar = decay[0:1]
    for f in range(FRAMES):
        if f:
            sofar = sofar * decay[f : f + 1]
        for h in range(HEADS):
            at = f * HEADS + h
            dec[at : at + 1, :] = jnp.broadcast_to(decay[f : f + 1, h : h + 1], (1, HD))
            reach[at : at + 1, :] = jnp.broadcast_to(sofar[:, h : h + 1], (1, HD))
    dsend[...] = jnp.concatenate(
        [reach[(FRAMES - 1) * HEADS :, :], jnp.zeros((8 - HEADS, HD), F32)], axis=0
    )

    valid = cam[...].astype(F32) * live
    lane = lax.broadcasted_iota(jnp.int32, (1, CAMS), 1)
    for n, c in enumerate((1, 2, 0, 3)):
        camera = ((lon * COLS + c) * CAMS) // LONG
        for f in range(FRAMES):
            bit = jnp.sum(jnp.where(lane == camera, valid[f : f + 1], 0.0), axis=1, keepdims=True)
            at = f * 2 * LAT + (n % 2) * LAT
            keep[n // 2, at : at + LAT, :] = jnp.broadcast_to(bit, (LAT, HD))

    def dec_copy(d):
        return pltpu.make_async_remote_copy(
            src_ref=dsend,
            dst_ref=tdec.at[slab],
            send_sem=dec_send.at[d],
            recv_sem=dec_recv.at[slab],
            device_id={"tm": slab + d},
            device_id_type=MESH,
        )

    x_rows = x_v.reshape(FRAMES * TOK, D)

    def halo_copy(side, f):
        target = (lon + (1 if side == 0 else LONS - 1)) % LONS
        return to_lon(
            edge_out.at[side, f],
            edge_in.at[side, f],
            halo_send.at[side, f],
            halo_recv.at[side, f],
            target,
        )

    for f in range(FRAMES):
        l_x[f].wait()

        def extract(j, f=f):
            lanes = pl.ds(pl.multiple_of(j * CHUNK, CHUNK), CHUNK)
            planes = dot(shift3[TOK + 2 * LAT : 2 * TOK, :], x_rows[f * TOK : (f + 1) * TOK, lanes])
            planes = planes.astype(BF16)
            edge_out[1, f, :, lanes] = planes[:LAT]
            edge_out[0, f, :, lanes] = planes[LAT:]

        repeat(0, D // CHUNK, extract, 6)
        if f == 0:
            pl.semaphore_wait(barrier, 2 * (LONS - 1))
        for side in range(2):
            halo_copy(side, f).start()
    repeat(1, SLABS - slab, lambda d: dec_copy(d).start())

    l_ck.wait()

    def taps(j):
        lanes = pl.ds(pl.multiple_of(j * CHUNK, CHUNK), CHUNK)
        k = [[0.5 * ck[i, n : n + 1, lanes] for n in range(3)] for i in range(3)]

        def one(f):
            x = x_rows[pl.ds(pl.multiple_of(f * TOK, TOK), TOK), lanes]
            s = [dot(shift3[i * TOK : (i + 1) * TOK, :], x) for i in range(3)]
            place = {1: 0, 2: 1, 0: 2, 3: 3}

            def plane(i, c):
                at = place[c] * LAT
                return s[i][at : at + LAT]

            at = pl.multiple_of(f * 2 * LAT, 2 * LAT)
            for n, c in enumerate((1, 2, 0, 3)):
                total = None
                for i in range(3):
                    for m in range(3):
                        if 0 <= c + m - 1 < COLS:
                            term = k[i][m] * plane(i, c + m - 1)
                            total = term if total is None else total + term
                rows = pl.ds(at + (n % 2) * LAT, LAT)
                if n < 2:
                    mixed[0, rows, lanes] = (total * jnp.tanh(total) + total).astype(BF16)
                else:
                    partial[rows, lanes] = total

        repeat(0, FRAMES, one, FRAMES)

    repeat(0, D // CHUNK, taps, 2)

    def project(side, first, count, weights, dst, masked, unroll):
        rows = pl.ds(first, count)

        def one(j):
            lanes = pl.ds(pl.multiple_of(j * CHUNK, CHUNK), CHUNK)
            r = dot(mixed[side, rows, :], weights[:, lanes])
            if masked:
                m = keep[side, rows, :]
                r = r * jnp.concatenate([m, m], axis=1)
            dst[side, rows, lanes] = r.astype(BF16)

        repeat(0, HK // CHUNK, one, unroll)

    l_wk.wait()
    project(0, 0, HALF, wk, k_v, True, 3)
    l_wv.wait()
    project(0, 0, HALF, wv, v_v, False, 3)

    def edge_taps(f):
        def one(j):
            lanes = pl.ds(pl.multiple_of(j * CHUNK, CHUNK), CHUNK)
            for side in range(2):
                s = dot(shift_h[...], edge_in[side, f, :, lanes])
                rows = pl.ds(f * 2 * LAT + side * LAT, LAT)
                total = partial[rows, lanes]
                for i in range(3):
                    tap = 0.5 * ck[i, 2 * side : 2 * side + 1, lanes]
                    total = total + tap * s[i * LAT : (i + 1) * LAT]
                mixed[1, rows, lanes] = (total * jnp.tanh(total) + total).astype(BF16)

        repeat(0, D // CHUNK, one, D // CHUNK)

    def scan_heads(frames, first, carried, put):
        def one(n):
            h = first + n
            lanes = pl.ds(pl.multiple_of(h * HD, HD), HD)
            at = pl.ds(pl.multiple_of(n * HD, HD), HD)
            total = None
            for f in frames:
                rows = pl.ds(f * 2 * LAT, 2 * LAT)
                keys = k_v[:, rows, lanes].reshape(TOK, HD)
                values = v_v[:, rows, lanes].reshape(TOK, HD)
                term = lax.dot_general(
                    keys, values, (((0,), (0,)), ((), ())), preferred_element_type=F32
                )
                if f:
                    before = carried[at, :] if total is None else total
                    term = term + dec[pl.ds(f * HEADS + h, 1), :] * before
                total = term
                put(f, at, total)
            carried[at, :] = total

        repeat(0, 3, one, 3)

    def put_other(f, at, total):
        other[f, at, :] = total.astype(BF16)

    def put_own(f, at, total):
        own[f, at, :] = total

    def frames_of(p):
        return pl.ds(PARTS[p][0], len(PARTS[p]))

    def a_copy(p):
        at = frames_of(p)
        return to_lon(other.at[at], abuf.at[at], a_send.at[p], a_recv.at[p], partner)

    def b_copy(p, d):
        to = (chip + d) % CHIPS
        rows = pl.ds(pl.multiple_of(to * PIECE, 16), PIECE)
        return to_lon(
            bsend.at[frames_of(p), rows],
            bbuf.at[d - 1, frames_of(p)],
            b_send.at[p, d],
            b_recv.at[p],
            2 * to + core,
        )

    def c_copy(p, d):
        held = states.at[pl.ds(*GATHERS[p]), pl.ds(mine, PIECE)]
        to = (chip + d) % CHIPS
        return to_lon(held, held, c_send.at[p, d], c_recv.at[p], 2 * to + core)

    def d_copy(p):
        held = states.at[pl.ds(*GATHERS[p]), pl.ds(half, OWN)]
        return to_lon(held, held, d_send.at[p], d_recv.at[p], partner)

    def t_copy(d):
        return pltpu.make_async_remote_copy(
            src_ref=tsend,
            dst_ref=tbuf.at[slab],
            send_sem=t_send.at[d],
            recv_sem=t_recv.at[slab],
            device_id={"tm": slab + d},
            device_id_type=MESH,
        )

    def after_a(p):
        a_copy(p).wait_recv()
        for f in PARTS[p]:
            for n in range(3):
                rows = pl.ds(n * HD, HD)
                total = own[f, rows, :] + abuf[f, rows, :].astype(F32)
                own[f, rows, :] = total
                bsend[f, rows, :] = total.astype(BF16)
        repeat(1, CHIPS, lambda d: b_copy(p, d).start())

    def after_b(p):
        wait_for(bbuf.at[:, frames_of(p)], b_recv.at[p])
        for f in PARTS[p]:
            total = own[f, pl.ds(mine_own, PIECE), :]
            for d in range(CHIPS - 1):
                total = total + bbuf[d, f].astype(F32)
            if f < EARLY:
                states[f, pl.ds(mine, PIECE), :] = total.astype(BF16)
            else:
                own[f, pl.ds(mine_own, PIECE), :] = total
            if f == FRAMES - 1:
                tsend[...] = total.astype(BF16)

    def send_c(p):
        repeat(1, CHIPS, lambda d: c_copy(p, d).start())

    def row_copy(at, k, sem):
        held = states.at[pl.ds(*GATHERS[0]), pl.ds(at, PIECE)]
        to = (chip // XS) * XS + (chip + k) % XS
        return to_lon(held, held, c_send.at[0, sem], c_recv.at[0], 2 * to + core)

    def across_copy():
        held = states.at[pl.ds(*GATHERS[0]), pl.ds(mine, PIECE)]
        to = (chip + XS) % CHIPS
        return to_lon(held, held, c_send.at[0, XS], across_recv, 2 * to + core)

    def send_early():
        across_copy().start()
        for k in range(1, XS):
            row_copy(mine, k, k).start()

    def pass_early():
        across_copy().wait_recv()
        at = pl.multiple_of(core * OWN + (chip + XS) % CHIPS * PIECE, 16)
        for k in range(1, XS):
            row_copy(at, k, XS + k).start()

    def after_c(p):
        pieces = OWN - PIECE if p else OWN - 2 * PIECE
        wait_for(states.at[pl.ds(*GATHERS[p]), pl.ds(0, pieces)], c_recv.at[p])
        d_copy(p).start()

    for group in ((0, 1), (2, 3)):
        for f in group:
            for side in range(2):
                halo_copy(side, f).wait_recv()
            edge_taps(f)
        first = group[0] * 2 * LAT
        if first:
            after_a(0)
        project(1, first, 4 * LAT, wk, k_v, True, 3)
        project(1, first, 4 * LAT, wv, v_v, False, 3)
        scan_heads(group, (1 - core) * 3, other_sum, put_other)
        if first:
            a_copy(1).start()
            a_copy(2).start()
        else:
            a_copy(0).start()
        scan_heads(group, core * 3, own_sum, put_own)
    after_a(1)
    after_a(2)
    after_b(0)
    send_early()
    after_b(1)
    for d in (4, 12, 5, 3, 11, 13, 2, 6, 10, 14, 8, 1, 7, 9, 15):

        @pl.when(slab + d < SLABS)
        def _(d=d):
            t_copy(d).start()

    after_b(2)
    l_wq.wait()
    project(0, 0, HALF, wq, q_v, False, 3)
    project(1, 0, HALF, wq, q_v, False, 3)

    first_head = mine_own // HD
    second_head = jnp.minimum(first_head + 1, 2)
    spot = lax.broadcasted_iota(jnp.int32, (PIECE, HD), 0) + mine_own
    in_first = spot < (first_head + 1) * HD

    def blank(n):
        weight[n] = jnp.zeros((PIECE, HD), F32)
        tbuf[n] = jnp.zeros((PIECE, HD), BF16)

    repeat(slab, SLABS, blank)

    def weigh(n, total):
        before = slab - 1 - n
        weight[before] = total
        wait_for(tdec.at[before], dec_recv.at[before])
        a = tdec[before, pl.ds(core * 3 + first_head, 1), :]
        b = tdec[before, pl.ds(core * 3 + second_head, 1), :]
        return jnp.where(in_first, a, b) * total

    lax.fori_loop(0, slab, weigh, jnp.ones((PIECE, HD), F32))
    pass_early()
    repeat(0, slab, lambda n: wait_for(tbuf.at[n], t_recv.at[n]))
    total = weight[0] * tbuf[0].astype(F32)
    for n in range(1, SLABS - 1):
        total = total + weight[n] * tbuf[n].astype(F32)
    states[FRAMES, pl.ds(mine, PIECE), :] = total.astype(BF16)
    for f in range(EARLY, FRAMES):
        a = reach[pl.ds(f * HEADS + core * 3 + first_head, 1), :]
        b = reach[pl.ds(f * HEADS + core * 3 + second_head, 1), :]
        state = own[f, pl.ds(mine_own, PIECE), :] + jnp.where(in_first, a, b) * total
        states[f, pl.ds(mine, PIECE), :] = state.astype(BF16)

    send_c(1)
    after_c(0)
    after_c(1)

    l_gain.wait()

    for h in range(HEADS):
        dec[h : h + 1, :] = gain[pl.ds(h * HD, HD)].reshape(1, HD)

    def read_heads(first):
        for f in range(FRAMES):
            rows = pl.ds(f * 2 * LAT, 2 * LAT)
            alive = jnp.where(f < n_live, 1.0, 0.0).astype(F32)
            for n in range(3):
                h = first + n
                at = pl.ds(pl.multiple_of(h * HD, HD), HD)
                state = states[f, at, :]
                if f < EARLY:
                    brought = reach[pl.ds(f * HEADS + h, 1), :] * states[FRAMES, at, :].astype(F32)
                    state = (state.astype(F32) + brought).astype(BF16)
                readout = dot(q_v[:, rows, at].reshape(TOK, HD), state)
                inverse = lax.rsqrt(jnp.mean(readout * readout, axis=-1, keepdims=True) + 1e-05)
                scale = dec[pl.ds(h, 1), :] * alive
                k_v[:, rows, at] = (readout * inverse * scale).astype(BF16).reshape(2, 2 * LAT, HD)

    read_heads(core * 3)
    for p in range(2):
        d_copy(p).wait_recv()
    read_heads((1 - core) * 3)
    for f in range(FRAMES):
        heads = k_v[:, pl.ds(f * 2 * LAT, 2 * LAT), :].reshape(TOK, HK)
        normed[f * TOK : (f + 1) * TOK, :] = dot(order[...], heads).astype(BF16)

    l_wo.wait()
    out_rows = out_v.reshape(FRAMES * TOK, D)

    def out_copy(j):
        lanes = pl.ds(pl.multiple_of(j * CHUNK, CHUNK), CHUNK)
        return pltpu.make_async_copy(
            out_v.at[:, :, :, lanes], out_hbm.at[:, :, :, lanes], out_sem.at[j]
        )

    def emit(j):
        lanes = pl.ds(pl.multiple_of(j * CHUNK, CHUNK), CHUNK)
        out_rows[:, lanes] = dot(normed[...], wo[:, lanes]).astype(BF16)
        out_copy(j).start()

    repeat(0, D // CHUNK, emit, 2)

    for f in range(FRAMES):
        for side in range(2):
            halo_copy(side, f).wait_send()
    for p in range(3):
        a_copy(p).wait_send()
        repeat(1, CHIPS, lambda d, p=p: b_copy(p, d).wait_send())
    for p in range(2):
        repeat(1, CHIPS, lambda d, p=p: c_copy(p, d).wait_send())
        d_copy(p).wait_send()
    repeat(1, SLABS - slab, lambda d: dec_copy(d).wait_send())
    repeat(1, SLABS - slab, lambda d: t_copy(d).wait_send())
    repeat(0, D // CHUNK, lambda j: out_copy(j).wait())


def out_kernel(in_hbm, out_hbm, held, in_sem, out_sem):
    fetches = [pltpu.make_async_copy(in_hbm.at[f], held.at[f], in_sem.at[f]) for f in range(FRAMES)]
    stores = [pltpu.make_async_copy(held.at[f], out_hbm.at[f], out_sem.at[f]) for f in range(FRAMES)]
    for copy in fetches:
        copy.start()
    for fetch, store in zip(fetches, stores):
        fetch.wait()
        store.start()
    for copy in stores:
        copy.wait()


def local(frames_in, conv_kernel, w_query, w_key, w_value, w_out, norm_gain, log_gate, cam_valid, live_frames):
    dma = pltpu.SemaphoreType.DMA
    anywhere = pl.BlockSpec(memory_space=pltpu.HBM)
    held = pl.BlockSpec(memory_space=pltpu.VMEM)
    result = pl.pallas_call(
        kernel,
        out_shape=jax.ShapeDtypeStruct((FRAMES, LAT, COLS, D), BF16),
        in_specs=[anywhere] * 10,
        out_specs=anywhere,
        scratch_shapes=[
            pltpu.SMEM((1,), jnp.int32),
            pltpu.VMEM((FRAMES, LAT, COLS, D), BF16),
            pltpu.VMEM((3, 3, D), F32),
            pltpu.VMEM((D, HK), BF16),
            pltpu.VMEM((D, HK), BF16),
            pltpu.VMEM((D, HK), BF16),
            pltpu.VMEM((HK, D), BF16),
            pltpu.VMEM((HK,), F32),
            pltpu.VMEM((FRAMES, HEADS), F32),
            pltpu.VMEM((FRAMES, CAMS), jnp.int32),
            pltpu.VMEM((3 * TOK, TOK), BF16),
            pltpu.VMEM((3 * LAT, LAT), BF16),
            pltpu.VMEM((TOK, TOK), BF16),
            pltpu.VMEM((2, FRAMES, LAT, D), BF16),
            pltpu.VMEM((2, FRAMES, LAT, D), BF16),
            pltpu.VMEM((HALF, D), F32),
            pltpu.VMEM((2, HALF, D), BF16),
            pltpu.VMEM((2, HALF, HK), BF16),
            pltpu.VMEM((2, HALF, HK), BF16),
            pltpu.VMEM((2, HALF, HK), BF16),
            pltpu.VMEM((2, HALF, HD), F32),
            pltpu.VMEM((FRAMES * HEADS, HD), F32),
            pltpu.VMEM((FRAMES * HEADS, HD), F32),
            pltpu.VMEM((FRAMES, OWN, HD), BF16),
            pltpu.VMEM((OWN, HD), F32),
            pltpu.VMEM((FRAMES, OWN, HD), F32),
            pltpu.VMEM((OWN, HD), F32),
            pltpu.VMEM((FRAMES, OWN, HD), BF16),
            pltpu.VMEM((FRAMES, OWN, HD), BF16),
            pltpu.VMEM((CHIPS - 1, FRAMES, PIECE, HD), BF16),
            pltpu.VMEM((PIECE, HD), BF16),
            pltpu.VMEM((SLABS, PIECE, HD), BF16),
            pltpu.VMEM((8, HD), F32),
            pltpu.VMEM((SLABS, 8, HD), F32),
            pltpu.VMEM((SLABS, PIECE, HD), F32),
            pltpu.VMEM((FRAMES + 1, HK, HD), BF16),
            pltpu.VMEM((FRAMES * TOK, HK), BF16),
            pltpu.VMEM((FRAMES, LAT, COLS, D), BF16),
            dma((13,)),
            dma((D // CHUNK,)),

            dma((2, FRAMES)),
            dma((2, FRAMES)),
            dma((3,)),
            dma((3,)),
            dma((3, CHIPS)),
            dma((3,)),
            dma((SLABS,)),
            dma((SLABS,)),
            dma((SLABS,)),
            dma((SLABS,)),
            dma((3, CHIPS)),
            dma((3,)),
            dma,
            dma((3,)),
            dma((3,)),
        ],
        compiler_params=pltpu.CompilerParams(
            collective_id=0, has_side_effects=True, vmem_limit_bytes=59392 * 1024
        ),
    )(frames_in, conv_kernel, w_query, w_key, w_value, w_out, norm_gain, log_gate, cam_valid, live_frames)
    return pl.pallas_call(
        out_kernel,
        out_shape=jax.ShapeDtypeStruct((FRAMES, LAT, COLS, D), BF16),
        in_specs=[anywhere],
        out_specs=anywhere,
        scratch_shapes=[
            pltpu.VMEM((FRAMES, LAT, COLS, D), BF16),
            dma((FRAMES,)),
            dma((FRAMES,)),
        ],
        compiler_params=pltpu.CompilerParams(vmem_limit_bytes=60 * 1024 * 1024),
    )(result)


def solution(mesh):
    in_specs = (
        P("tm", None, "lon", None),
        P(),
        P(),
        P(),
        P(),
        P(),
        P(),
        P("tm", None),
        P("tm", None),
        P("tm"),
    )
    out_specs = P("tm", None, "lon", None)
    return jax.shard_map(local, mesh=mesh, in_specs=in_specs, out_specs=out_specs, check_vma=False)
```
